256 devices in a mesh: dp: 16 (over z, core), ctx: 16 (over y, x).
Axes of the slice: x: 4, y: 4, z: 8, core: 2. Of those that a mesh axis runs over, the one named last changes fastest.
Arguments:
- layer_input: bfloat16 [16, 4096, 2048], P('dp', 'ctx'), may hold values from -6 to 6
- proj_weight: bfloat16 [2048, 256], replicated, may hold values from -0.005859375 to 0.005859375
- ssd_input: bfloat16 [16, 4096, 2048], P('dp', 'ctx'), may hold values from -0.3125 to 0.3125
- log_decay: bfloat16 [16, 4096, 32], P('dp', 'ctx'), may hold values from -2 to 0
- segment_ids: int32 [16, 4096], P('dp', 'ctx'), may hold values from 0 to 3, never falling along the last dimension, each value on 1 to 2048 neighbouring positions
- ssd_cotangent: bfloat16 [16, 4096, 2048], P('dp', 'ctx'), may hold values from -6 to 6
- window_qkv: bfloat16 [16, 4096, 3, 1024], P('dp', 'ctx'), may hold values from -8 to 8
Outputs:
- ssd_input_grad: bfloat16 [16, 4096, 2048], P('dp', 'ctx')
- proj_out_grad: bfloat16 [16, 4096, 256], P('dp', 'ctx')
- proj_weight_grad: float32 [2048, 256], replicated
- window_out: bfloat16 [16, 4096, 1024], P('dp', 'ctx')
The draws below stay inside these ranges and needn't reach their ends.
Inputs may be any that keep to these rules, and one draw needn't show every extreme that they name: `segment_ids`: within a sequence the ids never fall; each of the 4 documents holds 1 to 2048 tokens and one holds exactly 2048.
All inputs are finite; a program needn't handle non-finite values.
Results may differ from the reference program's by a relative error of at most 0.019.
Values may be sent and summed in bfloat16 or wider, within the bound.
No kernel may reach another device: no remote copies, remote signals or barrier semaphores. Data moves between devices by JAX's collectives and lax.ppermute only.
A program may use at most 192 MiB of HBM per device.

```python
import math
import jax
import jax.numpy as jnp
import numpy as np
from jax import lax

D = 2048
HALF_STATE_HEADS = 32
P_SIZE = 64
NST = 128
STRETCH = 256
HA = 16
HEAD = 64
WIN = 2048
DOCS = 4
TOK_DEV = 256
SEQUENCE_TOKENS = 4096
BATCH_SEQUENCES = 16


def draw_log_decay(key, part):
    key = jax.random.fold_in(key, 11)
    random_subkey_list = jax.random.split(key, 7)
    fast_share = 0.5
    choose = jax.random.uniform(random_subkey_list[0], (BATCH_SEQUENCES, 1, HALF_STATE_HEADS))
    fast_rate = 1.0 / jax.random.uniform(random_subkey_list[1], (BATCH_SEQUENCES, 1, HALF_STATE_HEADS), minval=30.0, maxval=50.0)
    slow_rate = jnp.exp(jax.random.uniform(random_subkey_list[2], (BATCH_SEQUENCES, 1, HALF_STATE_HEADS), minval=math.log(0.05), maxval=math.log(0.5))) * (math.log(10.0) / SEQUENCE_TOKENS)
    decay_speed = jnp.where(choose < fast_share, fast_rate, slow_rate)
    block_list = jnp.exp(jax.random.uniform(random_subkey_list[3], (BATCH_SEQUENCES, SEQUENCE_TOKENS // TOK_DEV, 1, HALF_STATE_HEADS), minval=-0.7, maxval=0.7))
    block_list = jnp.broadcast_to(block_list, (BATCH_SEQUENCES, SEQUENCE_TOKENS // TOK_DEV, TOK_DEV, HALF_STATE_HEADS)).reshape(BATCH_SEQUENCES, SEQUENCE_TOKENS, HALF_STATE_HEADS)
    jaggedness = jax.random.uniform(random_subkey_list[4], (BATCH_SEQUENCES, SEQUENCE_TOKENS, HALF_STATE_HEADS), minval=0.5, maxval=1.5)
    spike_places = jax.random.randint(random_subkey_list[5], (BATCH_SEQUENCES, 2, 1), 0, SEQUENCE_TOKENS)
    token_places = jnp.arange(SEQUENCE_TOKENS)[None, None, :]
    spike_mask = jnp.any(token_places == spike_places, axis=1)[:, :, None]
    spike_height = jax.random.uniform(random_subkey_list[6], (BATCH_SEQUENCES, SEQUENCE_TOKENS, HALF_STATE_HEADS), minval=math.log(0.5), maxval=math.log(0.8))
    drawn_values = jnp.where(spike_mask, spike_height, 0.0) - decay_speed * block_list * jaggedness
    return drawn_values.astype(jnp.float32).astype(jnp.bfloat16)


def draw_window_qkv(key, part):
    key = jax.random.fold_in(key, 23)
    random_subkey_list = jax.random.split(key, 1)
    full_shape = (BATCH_SEQUENCES, SEQUENCE_TOKENS, 3, HA * HEAD)
    drawn_values = jax.random.normal(random_subkey_list[0], full_shape)
    return drawn_values.astype(jnp.float32).astype(jnp.bfloat16)


def levels(rng, shape, cuts, smallest, top_value):
    def one(axis_at, parts):
        heights = jax.random.uniform(jax.random.fold_in(jax.random.fold_in(rng, 6), axis_at), (parts,), jnp.float32, smallest / len(cuts), top_value / len(cuts))
        return jnp.repeat(jnp.exp(heights), shape[axis_at] // parts).reshape((-1,) + (1,) * (len(shape) - axis_at - 1))

    level = one(*cuts[0])
    for cut in cuts[1:]:
        level = level * one(*cut)
    return level


def profile(amount, total, bound, skew):
    loads = [(1 << 20) // math.isqrt(grade ** skew) + 1 for grade in range(2, amount + 1)]
    rest, given = total - bound - (amount - 1), [1] * (amount - 1)
    while rest > 0:
        candidates = [i for i in range(amount - 1) if given[i] < bound]
        whole, left = sum([loads[i] for i in candidates]), rest
        for i in candidates:
            more = min(bound - given[i], max(1, left * loads[i] // whole), rest)
            given[i] = given[i] + more
            rest = rest - more
    return np.array([bound] + given)


def ragged(own_key, number_of, total, reach, slope):
    if number_of == 2:
        one = jax.random.randint(own_key, (), max(1, total - reach), min(reach, total - 1) + 1)
        return jnp.stack([one, total - one])
    tallies = jnp.asarray(profile(number_of, total, reach, slope), jnp.int32)
    pairs = (number_of - 1) // 2
    giver, receiver = tallies[1:1 + 2 * pairs:2], tallies[2:2 + 2 * pairs:2]
    room = jnp.minimum(giver - 1, reach - receiver)
    passed = jax.random.randint(jax.random.fold_in(own_key, 1), (pairs,), 0, 1 << 20) % (room + 1)
    tallies = tallies.at[1:1 + 2 * pairs:2].set(giver - passed).at[2:2 + 2 * pairs:2].set(receiver + passed)
    return tallies[jax.random.permutation(jax.random.fold_in(own_key, 2), number_of)]


def bell_draw(rng, dims, scale, limit, cuts=(), dtype=jnp.bfloat16):
    drawn = jax.random.normal(rng, dims, jnp.float32) * scale
    if len(cuts) > 0:
        drawn = levels(rng, dims, cuts, -0.22, 0.18) * drawn
    return jnp.clip(drawn, min=-limit, max=limit).astype(dtype)


def setup_inputs(seed: int = 0) -> dict:
    splits = jax.random.split(jax.random.key(seed), 8)
    return {
        "layer_input": bell_draw(splits[0], (BATCH_SEQUENCES, SEQUENCE_TOKENS, D), 1.0, 6.0, ((0, 16), (1, 16))),
        "proj_weight": bell_draw(splits[1], (D, 2 * NST), (D * 500) ** -0.5, 0.005859375),
        "ssd_input": bell_draw(splits[2], (BATCH_SEQUENCES, SEQUENCE_TOKENS, HALF_STATE_HEADS * P_SIZE), 0.02, 0.3125, ((0, 16), (1, 16))),
        "log_decay": draw_log_decay(jax.random.fold_in(splits[7], 71), 0),
        "segment_ids": jax.vmap(lambda own: jnp.searchsorted(jnp.cumsum(ragged(own, DOCS, SEQUENCE_TOKENS, SEQUENCE_TOKENS // 2, 0)), jnp.arange(SEQUENCE_TOKENS), side="right"))(jax.random.split(splits[4], BATCH_SEQUENCES)).reshape((BATCH_SEQUENCES, SEQUENCE_TOKENS)).astype(jnp.int32),
        "ssd_cotangent": bell_draw(splits[5], (BATCH_SEQUENCES, SEQUENCE_TOKENS, HALF_STATE_HEADS * P_SIZE), 1.0, 6.0, ((0, 16), (1, 16))),
        "window_qkv": draw_window_qkv(jax.random.fold_in(splits[7], 71), 0),
    }


full_precision = lax.Precision.HIGHEST

def stretch_terms(inputs, cotangents, b_rows, c_rows, decays, segments, prev_seg):
    running = jnp.cumsum(decays, axis=0)
    final_sum = running[-1]
    to_end = jnp.where((segments == segments[-1])[:, None], jnp.exp(final_sum[None, :] - running), 0.0)
    from_start = jnp.where((segments == prev_seg)[:, None], jnp.exp(running), 0.0)
    carry_gain = jnp.where(segments[-1] == prev_seg, jnp.exp(final_sum), 0.0)
    end_state = jnp.einsum('qn,qh,qhp->hnp', b_rows, to_end, inputs, precision=full_precision)
    start_grad = jnp.einsum('qn,qh,qhp->hnp', c_rows, from_start, cotangents, precision=full_precision)
    return (carry_gain, end_state, start_grad)

def stretch_grads(inputs, cotangents, b_rows, c_rows, decays, segments, prev_seg, entering, leaving):
    running = jnp.cumsum(decays, axis=0)
    final_sum = running[-1]
    to_end = jnp.where((segments == segments[-1])[:, None], jnp.exp(final_sum[None, :] - running), 0.0)
    from_start = jnp.where((segments == prev_seg)[:, None], jnp.exp(running), 0.0)
    places = jnp.arange(segments.shape[0])
    allowed = (places[:, None] >= places[None, :]) & (segments[:, None] == segments[None, :])
    log_gap = running.T[:, :, None] - running.T[:, None, :]
    decay_mask = jnp.where(allowed[None], jnp.exp(jnp.where(allowed[None], log_gap, 0.0)), 0.0)
    c_dot_b = jnp.dot(c_rows, b_rows.T, precision=full_precision)
    dot_rows = jnp.einsum('thp,shp->hts', cotangents, inputs, precision=full_precision)
    mixed_sum = lax.optimization_barrier(jnp.sum(decay_mask * dot_rows, axis=0))
    d_input = jnp.einsum('hts,thp->shp', decay_mask * c_dot_b[None], cotangents, precision=full_precision)
    d_input = d_input + jnp.einsum('sh,hnp,sn->shp', to_end, leaving, b_rows, precision=full_precision)
    grad_b = jnp.dot(mixed_sum.T, c_rows, precision=full_precision)
    grad_b = grad_b + jnp.einsum('sh,hnp,shp->sn', to_end, leaving, inputs, precision=full_precision)
    grad_c = jnp.dot(mixed_sum, b_rows, precision=full_precision)
    grad_c = grad_c + jnp.einsum('th,hnp,thp->tn', from_start, entering, cotangents, precision=full_precision)
    return (d_input, grad_b, grad_c)

def split_stretches(inputs, cotangents, b_rows, c_rows, decays, segments, prev_seg, block_len):
    length, head_count, head_width = inputs.shape
    block_count = length // block_len
    in_blocks = inputs.astype(jnp.float32).reshape(block_count, block_len, head_count, head_width)
    cot_blocks = cotangents.astype(jnp.float32).reshape(block_count, block_len, head_count, head_width)
    b_blocks = b_rows.astype(jnp.float32).reshape(block_count, block_len, -1)
    c_blocks = c_rows.astype(jnp.float32).reshape(block_count, block_len, -1)
    decay_blocks = decays.astype(jnp.float32).reshape(block_count, block_len, head_count)
    seg_blocks = segments.reshape(block_count, block_len)
    prev_segs = jnp.concatenate([jnp.reshape(prev_seg, (1,)).astype(jnp.int32), seg_blocks[:-1, -1]])
    return (in_blocks, cot_blocks, b_blocks, c_blocks, decay_blocks, seg_blocks, prev_segs)

def chain_before(carry_gain, end_state):

    def advance(carried, element):
        return ((carried[0] * element[0], element[0][:, None, None] * carried[1] + element[1]), carried)
    starting = (jnp.ones_like(carry_gain[0]), jnp.zeros_like(end_state[0]))
    return lax.scan(advance, starting, (carry_gain, end_state))

def chain_after(carry_gain, start_grad):

    def advance(carried, element):
        return ((carried[0] * element[0], element[1] + element[0][:, None, None] * carried[1]), carried)
    starting = (jnp.ones_like(carry_gain[0]), jnp.zeros_like(start_grad[0]))
    return lax.scan(advance, starting, (carry_gain, start_grad), reverse=True)

def stream_grads(pieces, before_pairs, after_pairs, entering, leaving):
    enter_all = before_pairs[1] + before_pairs[0][:, :, None, None] * entering[None]
    leave_all = after_pairs[1] + after_pairs[0][:, :, None, None] * leaving[None]

    def per_block(element):
        return stretch_grads(*element)
    d_input, grad_b, grad_c = lax.map(per_block, pieces + (enter_all, leave_all))
    block_count, block_len, head_count, head_width = pieces[0].shape
    total_rows = block_count * block_len
    return (d_input.reshape(total_rows, head_count, head_width), grad_b.reshape(total_rows, -1), grad_c.reshape(total_rows, -1))

def masked_probs(scores, allowed):
    masked = jnp.where(allowed[None], scores, -jnp.inf)
    row_max = lax.optimization_barrier(jnp.max(masked, axis=-1, keepdims=True))
    weights = jnp.exp(masked - row_max)
    return (weights / lax.optimization_barrier(jnp.sum(weights, axis=-1, keepdims=True))).astype(jnp.bfloat16)

def window_attention(queries, key_rows, value_rows, seg_ids):
    length, head_count, head_width = queries.shape
    blocked = math.gcd(length, 512)
    lead_rows = jnp.zeros((WIN, head_count, head_width), jnp.float32)
    padded_keys = jnp.concatenate([lead_rows, key_rows.astype(jnp.float32)])
    padded_values = jnp.concatenate([lead_rows, value_rows.astype(jnp.float32)])
    padded_ids = jnp.concatenate([jnp.full((WIN,), -1, jnp.int32), seg_ids])
    score_scale = head_width ** (-0.5)

    def per_block(offset):
        query_part = lax.dynamic_slice_in_dim(queries, offset, blocked, 0).astype(jnp.float32)
        key_part = lax.dynamic_slice_in_dim(padded_keys, offset, blocked + WIN, 0)
        value_part = lax.dynamic_slice_in_dim(padded_values, offset, blocked + WIN, 0)
        query_ids = lax.dynamic_slice_in_dim(seg_ids, offset, blocked, 0)
        key_ids = lax.dynamic_slice_in_dim(padded_ids, offset, blocked + WIN, 0)
        distance = (WIN + jnp.arange(blocked))[:, None] - jnp.arange(blocked + WIN)[None, :]
        allowed = (distance >= 0) & (distance < WIN) & (query_ids[:, None] == key_ids[None, :])
        scores = jnp.einsum('qhe,khe->hqk', query_part, key_part, precision=full_precision) * score_scale
        weights = masked_probs(scores, allowed).astype(jnp.float32)
        return jnp.einsum('hqk,khe->qhe', weights, value_part, precision=full_precision).astype(jnp.bfloat16)
    offsets = jnp.arange(length // blocked).astype(jnp.int32) * blocked
    return lax.map(per_block, offsets).reshape(length, head_count, head_width)

def reference(layer_input, proj_weight, ssd_input, log_decay, segment_ids, ssd_cotangent, window_qkv):

    def one_sequence(seq_index):
        inputs = layer_input[seq_index]
        seg_ids = segment_ids[seq_index]
        projected = jnp.dot(inputs, proj_weight, preferred_element_type=jnp.float32).astype(jnp.bfloat16)
        pieces = split_stretches(ssd_input[seq_index].reshape(SEQUENCE_TOKENS, HALF_STATE_HEADS, P_SIZE), ssd_cotangent[seq_index].reshape(SEQUENCE_TOKENS, HALF_STATE_HEADS, P_SIZE), projected[:, :NST], projected[:, NST:], log_decay[seq_index], seg_ids, jnp.int32(-1), STRETCH)
        carry_gain, end_state, start_grad = jax.vmap(stretch_terms)(*pieces)
        front_total, before_pairs = chain_before(carry_gain, end_state)
        back_total, after_pairs = chain_after(carry_gain, start_grad)
        no_state = jnp.zeros((HALF_STATE_HEADS, NST, P_SIZE), jnp.float32)
        d_input, grad_b, grad_c = stream_grads(pieces, before_pairs, after_pairs, no_state, no_state)
        out_grad = jnp.concatenate([grad_b, grad_c], axis=1).astype(jnp.bfloat16)
        partial_value = jnp.dot(inputs.T, out_grad, preferred_element_type=jnp.float32)
        qkv_rows = window_qkv[seq_index].reshape(SEQUENCE_TOKENS, 3, HA, HEAD)
        attended = window_attention(qkv_rows[:, 0], qkv_rows[:, 1], qkv_rows[:, 2], seg_ids)
        return (d_input.astype(jnp.bfloat16).reshape(SEQUENCE_TOKENS, HALF_STATE_HEADS * P_SIZE), out_grad, partial_value, attended.reshape(SEQUENCE_TOKENS, HA * HEAD))
    input_grads, out_grads, partials, attended_all = lax.map(one_sequence, jnp.arange(BATCH_SEQUENCES).astype(jnp.int32))
    weight_grad = lax.optimization_barrier(jnp.sum(partials, axis=0)) / math.sqrt(BATCH_SEQUENCES * SEQUENCE_TOKENS)
    return (input_grads, out_grads, weight_grad, attended_all)
```

```python
import math

import jax
import jax.numpy as jnp
from jax import lax
from jax.experimental import pallas as pl
from jax.experimental.pallas import tpu as pltpu
from jax.sharding import PartitionSpec as P

HEAD = 64
BIG = 16384.0
f32 = jnp.float32
bf16 = jnp.bfloat16
NT = (((1,), (1,)), ((), ()))


def mm(a, b):
    return jnp.dot(a, b, preferred_element_type=f32)


def mm_nt(a, b):
    return lax.dot_general(a, b, NT, preferred_element_type=f32)


def iota(shape, dim):
    return lax.broadcasted_iota(jnp.int32, shape, dim)


def ones_where(cond):
    return jnp.where(cond, 1.0, 0.0).astype(bf16)


def head_spread(heads, width, first):
    return ones_where(iota((heads, width), 0) == (iota((heads, width), 1) >> 6) + first)


def id_column(id_row):
    n = id_row.shape[1]
    eye = ones_where(iota((n, n), 0) == iota((n, n), 1))
    return mm_nt(eye, jnp.broadcast_to(id_row, (128, n)).astype(bf16))


def call(kernel, out_shape, *args, scratch=(), flops=0, n_bytes=4 << 20, prefetch=0):
    vmem = pl.BlockSpec(memory_space=pltpu.VMEM)
    smem = pl.BlockSpec(memory_space=pltpu.SMEM)
    many = isinstance(out_shape, (list, tuple))
    return pl.pallas_call(
        kernel,
        out_shape=out_shape,
        in_specs=[smem] * prefetch + [vmem] * (len(args) - prefetch),
        out_specs=[vmem] * len(out_shape) if many else vmem,
        scratch_shapes=list(scratch),
        compiler_params=pltpu.CompilerParams(vmem_limit_bytes=48 << 20),
        cost_estimate=pl.CostEstimate(flops=flops, bytes_accessed=n_bytes, transcendentals=0),
    )(*args)


def sds(shape, dtype):
    return jax.ShapeDtypeStruct(shape, dtype)


def states_kernel(inp, w, x, g, decay, ids, buf, proj_out, xs_out, gs_out, te_out):
    n_tok = inp.shape[0]
    heads = decay.shape[1]
    owners = buf.shape[0]
    proj = mm(inp[...], w[...]).astype(bf16)
    proj_out[...] = proj
    proj_t = proj.astype(f32).T.astype(bf16)
    half = proj.shape[1] // 2
    b_t, c_t = proj_t[:half], proj_t[half:]
    tri = ones_where(iota((n_tok, n_tok), 0) >= iota((n_tok, n_tok), 1))
    run = mm(tri, decay[...])
    final = run[n_tok - 1 : n_tok]
    id_row = ids[...].astype(f32)
    id_col = id_column(id_row)[:, :heads]
    first, last = id_col[:1], id_col[n_tok - 1 :]
    to_end = jnp.where(id_col == last, jnp.exp(final - run), 0.0).astype(bf16)
    from_start = jnp.where(id_col == first, jnp.exp(run), 0.0).astype(bf16)
    te_out[...] = to_end
    gain = jnp.where(first == last, jnp.exp(final), 0.0)
    gain_hi = gain.astype(bf16)
    gain_lo = (gain - gain_hi.astype(f32)).astype(bf16)
    gains = jnp.concatenate(
        [jnp.broadcast_to(gain_hi.astype(f32), (8, heads)), jnp.broadcast_to(gain_lo.astype(f32), (8, heads))]
    ).astype(bf16)
    row = iota((16, 128), 0)
    ends = jnp.where(row == 2, id_row[:, :1], id_row[:, n_tok - 1 :])
    for i in range(owners // 2):
        cols = slice(256 * i, 256 * i + 256)
        spread = head_spread(heads, 256, 4 * i)
        xs = (x[:, cols].astype(f32) * mm(to_end, spread)).astype(bf16)
        gs = (g[:, cols].astype(f32) * mm(from_start, spread)).astype(bf16)
        xs_out[:, cols] = xs
        gs_out[:, cols] = gs
        end_state = mm(b_t, xs).astype(bf16)
        start_grad = mm(c_t, gs).astype(bf16)
        gain_rows = mm(gains, spread)
        for k in range(2):
            part = slice(128 * k, 128 * k + 128)
            buf[2 * i + k, 0:128, :] = end_state[:, part]
            buf[2 * i + k, 128:256, :] = start_grad[:, part]
            meta = jnp.where(row == 0, gain_rows[0:1, part], jnp.where(row == 1, gain_rows[8:9, part], ends))
            buf[2 * i + k, 256:272, :] = meta.astype(bf16)


def chain_kernel(recv, send):
    count = recv.shape[0]
    meta = [recv[k, 256:272, :].astype(f32) for k in range(count)]
    gain = [m[0:1] + m[1:2] for m in meta]
    link = [jnp.zeros((1, 128), f32)]
    for k in range(1, count):
        link.append(jnp.where(meta[k][2:3] == meta[k - 1][3:4], 1.0, 0.0))
    state = jnp.zeros((128, 128), f32)
    for k in range(count):
        state = state * link[k]
        send[k, 0:128, :] = state.astype(bf16)
        state = state * gain[k] + recv[k, 0:128, :].astype(f32)
    adjoint = jnp.zeros((128, 128), f32)
    for k in range(count - 1, -1, -1):
        send[k, 128:256, :] = adjoint.astype(bf16)
        adjoint = (adjoint * gain[k] + recv[k, 128:256, :].astype(f32)) * link[k]


def intra_kernel(inp, proj, x, g, decay, ids, d_out, grad_out, inp_t, mixed):
    n_tok = inp.shape[0]
    heads = decay.shape[1]
    half = proj.shape[1] // 2
    square = (n_tok, n_tok)
    early, late = iota(square, 0), iota(square, 1)
    run = mm(ones_where(early >= late), decay[...])
    eye = ones_where(iota((heads, heads), 0) == iota((heads, heads), 1))
    decay_t = mm_nt(eye, decay[...]).astype(bf16)
    run_t = mm(decay_t, ones_where(early <= late))
    id_row = ids[...].astype(f32)
    id_col = id_column(id_row)[:, :1]
    bias = jnp.where((early <= late) & (id_col == id_row), 0.0, -1e30)
    b_rows, c_rows = proj[:, :half], proj[:, half:]
    b_dot_c = mm_nt(b_rows, c_rows)
    low_lane = iota((n_tok, 128), 1) < 64
    mixed[...] = jnp.zeros(square, f32)
    for p in range(heads // 2):
        cols = slice(128 * p, 128 * p + 128)
        xp, gp = x[:, cols], g[:, cols]
        zero = jnp.zeros_like(gp)
        total = jnp.zeros((n_tok, 128), f32)
        for k in range(2):
            h = 2 * p + k
            gh = jnp.where(low_lane, gp, zero) if k == 0 else jnp.where(low_lane, zero, gp)
            keep = jnp.exp(run_t[h : h + 1, :] - run[:, h : h + 1] + bias)
            mixed[...] += keep * mm_nt(xp, gh)
            total += mm((keep * b_dot_c).astype(bf16), gh)
        d_out[:, cols] = total
        inp_t[cols, :] = inp[:, cols].astype(f32).T.astype(bf16)
    both = mixed[...]
    grad_out[:, :half] = mm(both.astype(bf16), c_rows)
    grad_out[:, half:] = mm(both.T.astype(bf16), b_rows)


def outer_kernel(recv, xs, gs, grad_in, inp_t, og_out, share):
    owners = recv.shape[0]
    n_tok = xs.shape[0]
    grad_b = grad_in[:, :128]
    grad_c = grad_in[:, 128:]
    for i in range(owners // 2):
        cols = slice(256 * i, 256 * i + 256)
        enter = jnp.concatenate([recv[2 * i, 0:128, :], recv[2 * i + 1, 0:128, :]], axis=1)
        leave = jnp.concatenate([recv[2 * i, 128:256, :], recv[2 * i + 1, 128:256, :]], axis=1)
        grad_b += mm_nt(xs[:, cols], leave)
        grad_c += mm_nt(gs[:, cols], enter)
    og_out[:, :128] = grad_b.astype(bf16)
    og_out[:, 128:] = grad_c.astype(bf16)
    og = og_out[...]
    rows = inp_t.shape[0] // owners
    for j in range(owners):
        share[j] = mm(inp_t[rows * j : rows * j + rows, :], og).astype(bf16)


def input_grad_kernel(recv, proj, te, d_in, dx_out):
    owners = recv.shape[0]
    heads = te.shape[1]
    b_rows = proj[:, : proj.shape[1] // 2]
    for i in range(owners // 2):
        cols = slice(256 * i, 256 * i + 256)
        leave = jnp.concatenate([recv[2 * i, 128:256, :], recv[2 * i + 1, 128:256, :]], axis=1)
        spread = mm(te[...], head_spread(heads, 256, 4 * i))
        dx_out[:, cols] = (d_in[:, cols] + spread * mm(b_rows, leave)).astype(bf16)


def pack_kernel(qkv, ids, out):
    width = qkv.shape[1] // 3
    for m in range(3):
        for i in range(width // 128):
            at = m * width + 128 * i
            block = qkv[:, at : at + 128].astype(f32)
            if m == 0:
                block = block * HEAD ** (-0.5)
            turned = block.T.astype(bf16)
            out[2 * i, HEAD * m : HEAD * m + HEAD, :] = turned[:HEAD]
            out[2 * i + 1, HEAD * m : HEAD * m + HEAD, :] = turned[HEAD:]
    rows = jnp.broadcast_to(ids[...].astype(f32), (16, qkv.shape[0])).astype(bf16)
    for j in range(out.shape[0]):
        out[j, 192:208, :] = rows


def attention_kernel(lows, qkv, out, keys, values):
    blocks = qkv.shape[0]
    n = qkv.shape[2]
    slot = iota((16, n), 0).astype(f32)
    zeros48 = jnp.zeros((48, n), f32)
    pad_lane = iota((n, 128), 1)
    keys[0:n, :] = jnp.where((pad_lane >= 64) & (pad_lane < 80), -BIG, 0.0).astype(bf16)
    values[0] = jnp.zeros((80, n), bf16)

    def prepare(k, carry):
        ids = qkv[k, 192:208, :].astype(f32)
        other = jnp.where(ids == slot, 0.0, -BIG)
        tall = jnp.concatenate([qkv[k, 64:128, :].astype(f32), other, zeros48])
        keys[pl.ds(pl.multiple_of((k + 1) * n, n), n), :] = tall.T.astype(bf16)
        values[k + 1, 0:64, :] = qkv[k, 128:192, :]
        values[k + 1, 64:80, :] = jnp.ones((16, n), bf16)
        return carry

    lax.fori_loop(0, blocks, prepare, 0)
    future = jnp.where(iota((2 * n, n), 0) - n > iota((2 * n, n), 1), -BIG, 0.0)

    def per_block(b, carry):
        ids = qkv[b, 192:208, :].astype(f32)
        own = jnp.where(ids == slot, 1.0, 0.0)
        query = jnp.concatenate([qkv[b, 0:64, :].astype(f32), own, zeros48]).astype(bf16)

        def scores(at):
            return mm(keys[pl.ds(pl.multiple_of(at * n, n), 2 * n), :], query)

        def weighted(at, p):
            return mm(values[at], p[:n]) + mm(values[at + 1], p[n:])

        s = scores(b) + future
        top = jnp.max(s, axis=0, keepdims=True)
        total = weighted(b, jnp.exp(s - top).astype(bf16))

        def step(i, held):
            top, total = held
            at = b - 2 * i
            s = scores(at)
            new_top = jnp.maximum(top, jnp.max(s, axis=0, keepdims=True))
            p = jnp.exp(s - new_top).astype(bf16)
            return new_top, total * jnp.exp(top - new_top) + weighted(at, p)

        pairs = (b + 2 - lows[b]) // 2
        top, total = lax.fori_loop(1, pairs, step, (top, total))
        out[b] = (total[0:64] / total[64:65]).astype(bf16)
        return carry

    lax.fori_loop(0, blocks, per_block, 0)


def unpack_kernel(recv, out):
    for i in range(recv.shape[0] // 2):
        tall = jnp.concatenate([recv[2 * i], recv[2 * i + 1]]).astype(f32)
        out[:, 128 * i : 128 * i + 128] = tall.T.astype(bf16)


def exchange(blocks, axis):
    return lax.all_to_all(blocks, axis, split_axis=0, concat_axis=0, tiled=True)


def per_device(layer_input, proj_weight, ssd_input, log_decay, segment_ids, ssd_cotangent, window_qkv):
    inp, x, g = layer_input[0], ssd_input[0], ssd_cotangent[0]
    decay = log_decay[0]
    n_tok, width = inp.shape
    heads = decay.shape[1]
    ctx = lax.axis_size("ctx")
    dp = lax.axis_size("dp")
    n_out = proj_weight.shape[1]

    buf, proj, xs, gs, te = call(
        states_kernel,
        (
            sds((ctx, 272, 128), bf16),
            sds((n_tok, n_out), bf16),
            sds((n_tok, width), bf16),
            sds((n_tok, width), bf16),
            sds((n_tok, heads), bf16),
        ),
        inp, proj_weight, x, g, decay, segment_ids,
        flops=2 << 30, n_bytes=9 << 20,
    )
    got = exchange(buf, "ctx")

    packed = call(
        pack_kernel,
        sds((ctx, 208, n_tok), bf16),
        window_qkv.reshape(n_tok, -1), segment_ids,
        n_bytes=8 << 20,
    )
    rows = exchange(packed, "ctx")

    d_intra, grad_intra, inp_t = call(
        intra_kernel,
        (sds((n_tok, width), f32), sds((n_tok, n_out), f32), sds((width, n_tok), bf16)),
        inp, proj, x, g, decay, segment_ids,
        scratch=[pltpu.VMEM((n_tok, n_tok), f32)],
        flops=6 << 30, n_bytes=8 << 20,
    )
    back = exchange(call(chain_kernel, sds((ctx, 256, 128), bf16), got, n_bytes=6 << 20), "ctx")

    ids = rows[:, 192, :].astype(jnp.int32)
    lows = jnp.sum(ids[None, :, -1] < ids[:, None, 0], axis=1, dtype=jnp.int32)
    attended = call(
        attention_kernel,
        sds((ctx, HEAD, n_tok), bf16),
        lows, rows,
        scratch=[pltpu.VMEM(((ctx + 1) * n_tok, 128), bf16), pltpu.VMEM((ctx + 1, 80, n_tok), bf16)],
        flops=16 << 30, n_bytes=2 << 20, prefetch=1,
    )
    out_rows = exchange(attended, "ctx")

    out_grad, share = call(
        outer_kernel,
        (sds((n_tok, n_out), bf16), sds((ctx, width // ctx, n_out), bf16)),
        back, xs, gs, grad_intra, inp_t,
        flops=2 << 30, n_bytes=6 << 20,
    )
    shares = exchange(share, "ctx")
    part = jnp.sum(shares.astype(f32), axis=0).astype(bf16)
    parts = exchange(part.reshape(dp, -1, n_out), "dp")
    own = jnp.sum(parts.astype(f32), axis=0).astype(bf16)
    strip = exchange(jnp.broadcast_to(own[None], (dp,) + own.shape), "dp").reshape(part.shape)
    whole = exchange(jnp.broadcast_to(strip[None], (ctx,) + strip.shape), "ctx")
    weight_grad = whole.reshape(width, n_out).astype(f32) / math.sqrt(dp * ctx * n_tok)

    input_grad = call(
        input_grad_kernel, sds((n_tok, width), bf16), back, proj, te, d_intra, flops=1 << 30, n_bytes=4 << 20
    )
    window_out = call(unpack_kernel, sds((n_tok, ctx * HEAD), bf16), out_rows, n_bytes=1 << 20)
    return (input_grad[None], out_grad[None], weight_grad, window_out[None])


def solution(mesh):
    placed = (
        P("dp", "ctx", None),
        P(),
        P("dp", "ctx", None),
        P("dp", "ctx", None),
        P("dp", "ctx"),
        P("dp", "ctx", None),
        P("dp", "ctx", None, None),
    )
    return jax.shard_map(
        per_device,
        mesh=mesh,
        in_specs=placed,
        out_specs=(P("dp", "ctx", None), P("dp", "ctx", None), P(), P("dp", "ctx", None)),
        check_vma=False,
    )
```

```python
import functools
import math

import jax
import jax.numpy as jnp
from jax import lax
from jax.experimental import pallas as pl
from jax.experimental.pallas import tpu as pltpu
from jax.sharding import PartitionSpec as P

HEAD = 64
BIG = 16384.0
f32 = jnp.float32
bf16 = jnp.bfloat16
NT = (((1,), (1,)), ((), ()))


def mm(a, b):
    return jnp.dot(a, b, preferred_element_type=f32)


def mm_nt(a, b):
    return lax.dot_general(a, b, NT, preferred_element_type=f32)


def iota(shape, dim):
    return lax.broadcasted_iota(jnp.int32, shape, dim)


def ones_where(cond):
    return jnp.where(cond, 1.0, 0.0).astype(bf16)


def head_spread(heads, width, first):
    return ones_where(iota((heads, width), 0) == (iota((heads, width), 1) >> 6) + first)


def id_column(id_row):
    n = id_row.shape[1]
    eye = ones_where(iota((n, n), 0) == iota((n, n), 1))
    return mm_nt(eye, jnp.broadcast_to(id_row, (128, n)).astype(bf16))


def call(kernel, out_shape, *args, scratch=(), flops=0, n_bytes=4 << 20, prefetch=0, limit=24 << 20, hbm=(), out_hbm=False):
    vmem = pl.BlockSpec(memory_space=pltpu.VMEM)
    smem = pl.BlockSpec(memory_space=pltpu.SMEM)
    any_hbm = pl.BlockSpec(memory_space=pltpu.HBM)
    many = isinstance(out_shape, (list, tuple))
    return pl.pallas_call(
        kernel,
        out_shape=out_shape,
        in_specs=[smem if k < prefetch else any_hbm if k in hbm else vmem for k in range(len(args))],
        out_specs=[vmem] * len(out_shape) if many else any_hbm if out_hbm else vmem,
        scratch_shapes=list(scratch),
        compiler_params=pltpu.CompilerParams(vmem_limit_bytes=limit),
        cost_estimate=pl.CostEstimate(flops=flops, bytes_accessed=n_bytes, transcendentals=0),
    )(*args)


def sds(shape, dtype):
    return jax.ShapeDtypeStruct(shape, dtype)


def front_kernel(
    inp_hbm, w_hbm, x_hbm, g_hbm, qkv_hbm, decay_hbm, ids_hbm,
    buf_hbm, proj_out, te_out, fs_out,
    inp, w, x, g, qkv, decay_t, ids, buf, in_sem, part_sem, out_sem,
):
    n_tok, width = inp.shape
    heads = decay_t.shape[0]
    owners = buf.shape[0]
    whole = [
        pltpu.make_async_copy(src, dst, in_sem.at[k])
        for k, (src, dst) in enumerate(
            [(decay_hbm, decay_t), (ids_hbm, ids)]
            + [(qkv_hbm.at[m], qkv.at[m]) for m in range(3)]
            + [
                (src.at[:, pl.ds(width // 4 * q, width // 4)], dst.at[:, pl.ds(width // 4 * q, width // 4)])
                for q in range(4)
                for src, dst in ((x_hbm, x), (g_hbm, g))
            ]
        )
    ]
    chunk = width // 4
    parts = []
    for k in range(4):
        at = pl.ds(chunk * k, chunk)
        parts.append(
            (
                pltpu.make_async_copy(inp_hbm.at[:, at], inp.at[:, at], part_sem.at[0, k]),
                pltpu.make_async_copy(w_hbm.at[at, :], w.at[at, :], part_sem.at[1, k]),
            )
        )
    whole[0].start()
    whole[1].start()
    for pair in parts:
        pair[0].start()
        pair[1].start()
    for copy in whole[5:] + whole[2:5]:
        copy.start()

    early, late = iota((n_tok, n_tok), 0), iota((n_tok, n_tok), 1)
    tri = ones_where(early >= late)
    whole[0].wait()
    whole[1].wait()
    run = mm_nt(tri, decay_t[...])
    final = run[n_tok - 1 : n_tok]
    id_row = ids[...].astype(f32)
    id_col = id_column(id_row)[:, :heads]
    first, last = id_col[:1], id_col[n_tok - 1 :]
    to_end = jnp.where(id_col == last, jnp.exp(final - run), 0.0).astype(bf16)
    from_start = jnp.where(id_col == first, jnp.exp(run), 0.0).astype(bf16)
    te_out[...] = to_end
    fs_out[...] = from_start
    gain = jnp.where(first == last, jnp.exp(final), 0.0)
    gain_hi = gain.astype(bf16)
    gain_lo = (gain - gain_hi.astype(f32)).astype(bf16)
    gains = jnp.concatenate(
        [jnp.broadcast_to(gain_hi.astype(f32), (8, heads)), jnp.broadcast_to(gain_lo.astype(f32), (8, heads))]
    ).astype(bf16)
    row = iota((16, 256), 0)
    ends = jnp.where(row == 0, id_row, jnp.where(row == 3, id_row[:, :1], id_row[:, n_tok - 1 :]))

    total = jnp.zeros((n_tok, w.shape[1]), f32)
    for k in range(4):
        at = slice(chunk * k, chunk * k + chunk)
        parts[k][0].wait()
        parts[k][1].wait()
        total += mm(inp[:, at], w[at, :])
    proj = total.astype(bf16)
    proj_out[...] = proj
    proj_t = proj.astype(f32).T.astype(bf16)
    half = proj.shape[1] // 2
    b_t, c_t = proj_t[:half], proj_t[half:]
    sends = []
    for i in range(owners // 2):
        if i % 2 == 0:
            whole[5 + i].wait()
            whole[6 + i].wait()
        cols = slice(256 * i, 256 * i + 256)
        spread = head_spread(heads, 256, 4 * i)
        xs = (x[:, cols].astype(f32) * mm(to_end, spread)).astype(bf16)
        gs = (g[:, cols].astype(f32) * mm(from_start, spread)).astype(bf16)
        end_state = mm(b_t, xs).astype(bf16)
        start_grad = mm(c_t, gs).astype(bf16)
        gain_rows = mm(gains, spread)
        for k in range(2):
            part = slice(128 * k, 128 * k + 128)
            buf[2 * i + k, 0:128, 0:128] = end_state[:, part]
            buf[2 * i + k, 0:128, 128:256] = start_grad[:, part]
            gain_hi_row = jnp.concatenate([gain_rows[0:1, part]] * 2, axis=1)
            gain_lo_row = jnp.concatenate([gain_rows[8:9, part]] * 2, axis=1)
            meta = jnp.where(row == 1, gain_hi_row, jnp.where(row == 2, gain_lo_row, ends))
            buf[2 * i + k, 128:144, :] = meta.astype(bf16)
        span = (pl.ds(2 * i, 2), pl.ds(0, 144))
        sends.append(pltpu.make_async_copy(buf.at[span], buf_hbm.at[span], out_sem.at[0, i]))
        sends[-1].start()
    for m in range(3):
        whole[2 + m].wait()
    for i in range(owners // 2):
        for m in range(3):
            block = qkv[m, :, 128 * i : 128 * i + 128].astype(f32)
            if m == 0:
                block = block * HEAD ** (-0.5)
            turned = block.T.astype(bf16)
            at = slice(144 + HEAD * m, 144 + HEAD * m + HEAD)
            buf[2 * i, at, :] = turned[:HEAD]
            buf[2 * i + 1, at, :] = turned[HEAD:]
        span = (pl.ds(2 * i, 2), pl.ds(144, 192))
        sends.append(pltpu.make_async_copy(buf.at[span], buf_hbm.at[span], out_sem.at[1, i]))
        sends[-1].start()
    for copy in sends:
        copy.wait()


def chain_kernel(recv, after, send_hbm, send, sem):
    count = recv.shape[0]
    meta = [recv[k, 128:144, :].astype(f32) for k in range(count)]
    gain = [m[1:2, :128] + m[2:3, :128] for m in meta]
    link = [jnp.zeros((1, 128), f32)]
    for k in range(1, count):
        link.append(jnp.where(meta[k][3:4, :128] == meta[k - 1][4:5, :128], 1.0, 0.0))
    state = jnp.zeros((128, 128), f32)
    for k in range(count):
        state = state * link[k]
        send[k, :, 0:128] = state.astype(bf16)
        state = state * gain[k] + recv[k, 0:128, 0:128].astype(f32)
    adjoint = jnp.zeros((128, 128), f32)
    copies = []
    for k in range(count - 1, -1, -1):
        send[k, :, 128:256] = adjoint.astype(bf16)
        copies.append(pltpu.make_async_copy(send.at[k], send_hbm.at[k], sem.at[k]))
        copies[-1].start()
        adjoint = (adjoint * gain[k] + recv[k, 0:128, 128:256].astype(f32)) * link[k]
    for copy in copies:
        copy.wait()


def intra_kernel(inp, proj, x, g, te, fs, decay_t, ids, d_out, grad_out, kept, done, mixed):
    done[...] = jnp.zeros(done.shape, f32)
    n_tok = inp.shape[0]
    heads = decay_t.shape[0]
    half = proj.shape[1] // 2
    square = (n_tok, n_tok)
    early, late = iota(square, 0), iota(square, 1)
    run = mm_nt(ones_where(early >= late), decay_t[...])
    run_t = mm(decay_t[...], ones_where(early <= late))
    id_row = ids[...].astype(f32)
    id_col = id_column(id_row)[:, :1]
    bias = jnp.where((early <= late) & (id_col == id_row), 0.0, -1e30)
    b_rows, c_rows = proj[:, :half], proj[:, half:]
    b_dot_c = mm_nt(b_rows, c_rows)
    low_lane = iota((n_tok, 128), 1) < 64
    mixed[...] = jnp.zeros(square, f32)
    for p in range(heads // 2):
        cols = slice(128 * p, 128 * p + 128)
        xp, gp = x[:, cols], g[:, cols]
        zero = jnp.zeros_like(gp)
        total = jnp.zeros((n_tok, 128), f32)
        for k in range(2):
            h = 2 * p + k
            gh = jnp.where(low_lane, gp, zero) if k == 0 else jnp.where(low_lane, zero, gp)
            keep = jnp.exp(run_t[h : h + 1, :] - run[:, h : h + 1] + bias)
            mixed[...] += keep * mm_nt(xp, gh)
            total += mm((keep * b_dot_c).astype(bf16), gh)
        d_out[:, cols] = total
        spread = head_spread(heads, 128, 2 * p)
        rows = slice(n_tok * (p // 2), n_tok * (p // 2) + n_tok)
        side = slice(128 * (p % 2), 128 * (p % 2) + 128)
        kept[0, rows, side] = (xp.astype(f32) * mm(te[...], spread)).astype(bf16)
        kept[1, rows, side] = (gp.astype(f32) * mm(fs[...], spread)).astype(bf16)
        kept[2, cols, :] = inp[:, cols].astype(f32).T.astype(bf16)
    both = mixed[...]
    grad_out[:, :half] = mm(both.astype(bf16), c_rows)
    grad_out[:, half:] = mm(both.T.astype(bf16), b_rows)


def outer_kernel(core, recv_hbm, kept_hbm, grad_in, after, og_out, keep, give, recv, kept, sem):
    owners = recv.shape[0]
    n_tok = grad_in.shape[0]
    copies, arrivals = [], []
    for q in range(4):
        rows = pl.ds(kept.shape[1] // 4 * q, kept.shape[1] // 4)
        for k in range(2):
            copies.append(pltpu.make_async_copy(kept_hbm.at[k, rows], kept.at[k, rows], sem.at[2 * q + k]))
        span = pl.ds(owners // 4 * q, owners // 4)
        arrivals.append(pltpu.make_async_copy(recv_hbm.at[span], recv.at[span], sem.at[9 + q]))
        arrivals[-1].start()
        copies[2 * q].start()
        copies[2 * q + 1].start()
    copies.append(pltpu.make_async_copy(kept_hbm.at[2], kept.at[2], sem.at[8]))
    copies[8].start()
    grad_b = grad_in[:, :128]
    grad_c = grad_in[:, 128:]
    for i in range(owners // 2):
        if i % 2 == 0:
            copies[i].wait()
            copies[i + 1].wait()
            arrivals[i // 2].wait()
        rows = slice(n_tok * i, n_tok * i + n_tok)
        enter = jnp.concatenate([recv[2 * i, :, 0:128], recv[2 * i + 1, :, 0:128]], axis=1)
        leave = jnp.concatenate([recv[2 * i, :, 128:256], recv[2 * i + 1, :, 128:256]], axis=1)
        grad_b += mm_nt(kept[0, rows, :], leave)
        grad_c += mm_nt(kept[1, rows, :], enter)
    og_out[:, :128] = grad_b.astype(bf16)
    og_out[:, 128:] = grad_c.astype(bf16)
    og = og_out[...]
    copies[8].wait()
    rows = kept.shape[1] // owners // 2
    mine = pl.multiple_of(core[0] * rows, rows)
    other = pl.multiple_of(rows - core[0] * rows, rows)
    for j in range(owners):
        keep[j] = mm(kept[2, pl.ds(2 * rows * j + mine, rows), :], og)
        give[j] = mm(kept[2, pl.ds(2 * rows * j + other, rows), :], og).astype(bf16)


def input_grad_kernel(recv, proj, te, d_in, dx_out, done):
    done[...] = jnp.zeros(done.shape, f32)
    owners = recv.shape[0]
    heads = te.shape[1]
    b_rows = proj[:, : proj.shape[1] // 2]
    for i in range(owners // 2):
        cols = slice(256 * i, 256 * i + 256)
        leave = jnp.concatenate([recv[2 * i, :, 128:256], recv[2 * i + 1, :, 128:256]], axis=1)
        spread = mm(te[...], head_spread(heads, 256, 4 * i))
        dx_out[:, cols] = (d_in[:, cols] + spread * mm(b_rows, leave)).astype(bf16)


def attention_kernel(lows, qkv, out, done, keys, values):
    done[...] = jnp.zeros(done.shape, f32)
    blocks = qkv.shape[0]
    n = qkv.shape[2]
    slot = iota((16, n), 0).astype(f32)
    zeros48 = jnp.zeros((48, n), f32)

    def prepare(k, carry):
        ids = qkv[k, 128:144, :].astype(f32)[0:1]
        other = jnp.where(ids == slot, 0.0, -BIG)
        tall = jnp.concatenate([qkv[k, 208:272, :].astype(f32), other, zeros48])
        keys[pl.ds(pl.multiple_of(k * n, n), n), :] = tall.T.astype(bf16)
        values[k, 0:64, :] = qkv[k, 272:336, :]
        values[k, 64:80, :] = jnp.ones((16, n), bf16)
        return carry

    lax.fori_loop(0, blocks, prepare, 0)
    later = iota((2 * n, n), 0) - iota((2 * n, n), 1)
    masks = [jnp.where(later > k * n, -BIG, 0.0) for k in range(2)]

    def per_pair(c, carry):
        queries = []
        for k in range(2):
            ids = qkv[2 * c + k, 128:144, :].astype(f32)[0:1]
            own = jnp.where(ids == slot, 1.0, 0.0)
            rows = qkv[2 * c + k, 144:208, :].astype(f32)
            queries.append(jnp.concatenate([rows, own, zeros48]).astype(bf16))

        def scores(at, query):
            return mm(keys[pl.ds(pl.multiple_of(at * n, n), 2 * n), :], query)

        def weighted(at, p):
            return mm(values[at], p[:n]) + mm(values[at + 1], p[n:])

        held = []
        for k in range(2):
            s = scores(2 * c, queries[k]) + masks[k]
            top = jnp.max(s, axis=0, keepdims=True)
            held += [top, weighted(2 * c, jnp.exp(s - top).astype(bf16))]

        def step(i, held):
            at = 2 * (c - i)
            new = []
            s = [scores(at, query) for query in queries]
            for k in range(2):
                top, total = held[2 * k], held[2 * k + 1]
                new_top = jnp.maximum(top, jnp.max(s[k], axis=0, keepdims=True))
                p = jnp.exp(s[k] - new_top).astype(bf16)
                new += [new_top, total * jnp.exp(top - new_top) + weighted(at, p)]
            return tuple(new)

        held = lax.fori_loop(1, c + 1 - lows[2 * c] // 2, step, tuple(held))
        for k in range(2):
            total = held[2 * k + 1]
            out[2 * c + k] = (total[0:64] / total[64:65]).astype(bf16)
        return carry

    lax.fori_loop(0, blocks // 2, per_pair, 0)


def unpack_kernel(recv, out, done):
    done[...] = jnp.zeros(done.shape, f32)
    for i in range(recv.shape[0] // 2):
        tall = jnp.concatenate([recv[2 * i, 64:128], recv[2 * i + 1, 64:128]]).astype(f32)
        out[:, 128 * i : 128 * i + 128] = tall.T.astype(bf16)


def sum_kernel(recv, after, out):
    rows = out.shape[1]
    total = recv[0, 0:rows, :].astype(f32)
    for k in range(1, recv.shape[0]):
        total += recv[k, 0:rows, :].astype(f32)
    total = total.astype(bf16)
    for k in range(out.shape[0]):
        out[k] = total


def assemble_kernel(core, mine, other, out, *, scale):
    for j in range(out.shape[0]):
        out[j, core[0]] = mine[j].astype(f32) * scale
        out[j, 1 - core[0]] = other[j].astype(f32) * scale


def exchange(blocks, axis, groups=None):
    return lax.all_to_all(blocks, axis, split_axis=0, concat_axis=0, tiled=True, axis_index_groups=groups)


def per_device(layer_input, proj_weight, ssd_input, log_decay, segment_ids, ssd_cotangent, window_qkv):
    inp, x, g = layer_input[0], ssd_input[0], ssd_cotangent[0]
    decay_t = log_decay[0].T
    qkv = window_qkv[0].transpose(1, 0, 2)
    n_tok, width = inp.shape
    heads = decay_t.shape[0]
    ctx = lax.axis_size("ctx")
    dp = lax.axis_size("dp")
    n_out = proj_weight.shape[1]
    core = lax.axis_index("dp") % 2
    pairs = [(i, i ^ 1) for i in range(dp)]
    planes = [list(range(c, dp, 2)) for c in range(2)]

    done = sds((8, 128), f32)

    vmem = pl.BlockSpec(memory_space=pltpu.VMEM)
    anywhere = pl.BlockSpec(memory_space=pltpu.HBM)
    buf, proj, te, fs = pl.pallas_call(
        front_kernel,
        out_shape=(
            sds((ctx, 336, n_tok), bf16),
            sds((n_tok, n_out), bf16),
            sds((n_tok, heads), bf16),
            sds((n_tok, heads), bf16),
        ),
        in_specs=[anywhere] * 7,
        out_specs=(anywhere, vmem, vmem, vmem),
        scratch_shapes=[
            pltpu.VMEM(a.shape, a.dtype) for a in (inp, proj_weight, x, g, qkv, decay_t, segment_ids)
        ]
        + [
            pltpu.VMEM((ctx, 336, n_tok), bf16),
            pltpu.SemaphoreType.DMA((13,)),
            pltpu.SemaphoreType.DMA((2, 4)),
            pltpu.SemaphoreType.DMA((2, ctx // 2)),
        ],
        compiler_params=pltpu.CompilerParams(vmem_limit_bytes=64 << 20),
        cost_estimate=pl.CostEstimate(flops=2 << 30, bytes_accessed=9 << 20, transcendentals=0),
    )(inp, proj_weight, x, g, qkv, decay_t, segment_ids)
    got = exchange(buf, "ctx")

    d_intra, grad_intra, kept, intra_done = call(
        intra_kernel,
        (
            sds((n_tok, width), f32),
            sds((n_tok, n_out), f32),
            sds((3, width, n_tok), bf16),
            done,
        ),
        inp, proj, x, g, te, fs, decay_t, segment_ids,
        scratch=[pltpu.VMEM((n_tok, n_tok), f32)],
        flops=6 << 30, n_bytes=8 << 20,
    )
    sent = call(
        chain_kernel,
        sds((ctx, 128, 256), bf16),
        got, intra_done,
        scratch=[pltpu.VMEM((ctx, 128, 256), bf16), pltpu.SemaphoreType.DMA((ctx,))],
        n_bytes=6 << 20, limit=24 << 20, out_hbm=True,
    )
    back = exchange(sent, "ctx")

    ids = got[:, 128, :].astype(jnp.int32)
    lows = jnp.sum(ids[None, :, -1] < ids[:, None, 0], axis=1, dtype=jnp.int32)
    attended, attention_done = call(
        attention_kernel,
        (sds((ctx, HEAD, n_tok), bf16), done),
        lows, got,
        scratch=[pltpu.VMEM((ctx * n_tok, 128), bf16), pltpu.VMEM((ctx, 80, n_tok), bf16)],
        flops=16 << 30, n_bytes=2 << 20, prefetch=1,
    )

    half_rows = width // ctx // 2
    out_grad, keep, give = call(
        outer_kernel,
        (sds((n_tok, n_out), bf16), sds((ctx, half_rows, n_out), f32), sds((ctx, half_rows, n_out), bf16)),
        core[None], back, kept, grad_intra, attention_done,
        scratch=[
            pltpu.VMEM((ctx, 128, 256), bf16),
            pltpu.VMEM((3, width, n_tok), bf16),
            pltpu.SemaphoreType.DMA((13,)),
        ],
        flops=2 << 30, n_bytes=6 << 20, prefetch=1, limit=62 << 20, hbm=(1, 2),
    )
    share = (keep + lax.ppermute(give, "dp", pairs).astype(f32)).astype(bf16)
    third = exchange(jnp.concatenate([share, attended], axis=1), "ctx")
    input_grad, input_done = call(
        input_grad_kernel,
        (sds((n_tok, width), bf16), done),
        back, proj, te, d_intra,
        flops=1 << 30, n_bytes=4 << 20,
    )
    part = call(sum_kernel, sds((dp // 2, half_rows, n_out), bf16), third, input_done, n_bytes=2 << 20)
    parts = exchange(part, "dp", planes)
    window_out, window_done = call(
        unpack_kernel, (sds((n_tok, ctx * HEAD), bf16), done), third, n_bytes=1 << 20
    )
    strip = call(sum_kernel, sds((ctx, half_rows, n_out), bf16), parts, window_done, n_bytes=1 << 20)
    mine = exchange(strip, "ctx")
    other = lax.ppermute(mine, "dp", pairs)
    weight_grad = call(
        functools.partial(assemble_kernel, scale=1.0 / math.sqrt(dp * ctx * n_tok)),
        sds((ctx, 2, half_rows, n_out), f32),
        core[None], mine, other,
        n_bytes=4 << 20, prefetch=1,
    ).reshape(width, n_out)
    return (input_grad[None], out_grad[None], weight_grad, window_out[None])


def solution(mesh):
    placed = (
        P("dp", "ctx", None),
        P(),
        P("dp", "ctx", None),
        P("dp", "ctx", None),
        P("dp", "ctx"),
        P("dp", "ctx", None),
        P("dp", "ctx", None, None),
    )
    return jax.shard_map(
        per_device,
        mesh=mesh,
        in_specs=placed,
        out_specs=(P("dp", "ctx", None), P("dp", "ctx", None), P(), P("dp", "ctx", None)),
        check_vma=False,
    )
```

```python
import functools
import math

import jax
import jax.numpy as jnp
from jax import lax
from jax.experimental import pallas as pl
from jax.experimental.pallas import tpu as pltpu
from jax.sharding import PartitionSpec as P

HEAD = 64
BIG = 16384.0
f32 = jnp.float32
bf16 = jnp.bfloat16
NT = (((1,), (1,)), ((), ()))


def mm(a, b):
    return jnp.dot(a, b, preferred_element_type=f32)


def mm_nt(a, b):
    return lax.dot_general(a, b, NT, preferred_element_type=f32)


def iota(shape, dim):
    return lax.broadcasted_iota(jnp.int32, shape, dim)


def ones_where(cond):
    return jnp.where(cond, 1.0, 0.0).astype(bf16)


def head_spread(heads, width, first):
    return ones_where(iota((heads, width), 0) == (iota((heads, width), 1) >> 6) + first)


def id_column(id_row):
    n = id_row.shape[1]
    eye = ones_where(iota((n, n), 0) == iota((n, n), 1))
    return mm_nt(eye, jnp.broadcast_to(id_row, (128, n)).astype(bf16))


def call(kernel, out_shape, *args, scratch=(), flops=0, n_bytes=4 << 20, prefetch=0, limit=24 << 20, hbm=()):
    vmem = pl.BlockSpec(memory_space=pltpu.VMEM)
    smem = pl.BlockSpec(memory_space=pltpu.SMEM)
    any_hbm = pl.BlockSpec(memory_space=pltpu.HBM)
    many = isinstance(out_shape, (list, tuple))
    return pl.pallas_call(
        kernel,
        out_shape=out_shape,
        in_specs=[smem if k < prefetch else any_hbm if k in hbm else vmem for k in range(len(args))],
        out_specs=[vmem] * len(out_shape) if many else vmem,
        scratch_shapes=list(scratch),
        compiler_params=pltpu.CompilerParams(vmem_limit_bytes=limit),
        cost_estimate=pl.CostEstimate(flops=flops, bytes_accessed=n_bytes, transcendentals=0),
    )(*args)


def sds(shape, dtype):
    return jax.ShapeDtypeStruct(shape, dtype)


def front_kernel(
    inp_hbm, w_hbm, x_hbm, g_hbm, qkv_hbm, decay_hbm, ids_hbm,
    buf_hbm, proj_out, te_out, fs_out,
    inp, w, x, g, qkv, decay_t, ids, buf, in_sem, part_sem, out_sem,
):
    n_tok, width = inp.shape
    heads = decay_t.shape[0]
    owners = buf.shape[0]
    whole = [
        pltpu.make_async_copy(src, dst, in_sem.at[k])
        for k, (src, dst) in enumerate(
            [(decay_hbm, decay_t), (ids_hbm, ids)]
            + [(qkv_hbm.at[m], qkv.at[m]) for m in range(3)]
            + [
                (src.at[:, pl.ds(width // 4 * q, width // 4)], dst.at[:, pl.ds(width // 4 * q, width // 4)])
                for q in range(4)
                for src, dst in ((x_hbm, x), (g_hbm, g))
            ]
        )
    ]
    chunk = width // 4
    parts = []
    for k in range(4):
        at = pl.ds(chunk * k, chunk)
        parts.append(
            (
                pltpu.make_async_copy(inp_hbm.at[:, at], inp.at[:, at], part_sem.at[0, k]),
                pltpu.make_async_copy(w_hbm.at[at, :], w.at[at, :], part_sem.at[1, k]),
            )
        )
    whole[0].start()
    whole[1].start()
    for pair in parts:
        pair[0].start()
        pair[1].start()
    for copy in whole[5:] + whole[2:5]:
        copy.start()

    early, late = iota((n_tok, n_tok), 0), iota((n_tok, n_tok), 1)
    tri = ones_where(early >= late)
    whole[0].wait()
    whole[1].wait()
    run = mm_nt(tri, decay_t[...])
    final = run[n_tok - 1 : n_tok]
    id_row = ids[...].astype(f32)
    id_col = id_column(id_row)[:, :heads]
    first, last = id_col[:1], id_col[n_tok - 1 :]
    to_end = jnp.where(id_col == last, jnp.exp(final - run), 0.0).astype(bf16)
    from_start = jnp.where(id_col == first, jnp.exp(run), 0.0).astype(bf16)
    te_out[...] = to_end
    fs_out[...] = from_start
    gain = jnp.where(first == last, jnp.exp(final), 0.0)
    gain_hi = gain.astype(bf16)
    gain_lo = (gain - gain_hi.astype(f32)).astype(bf16)
    gains = jnp.concatenate(
        [jnp.broadcast_to(gain_hi.astype(f32), (8, heads)), jnp.broadcast_to(gain_lo.astype(f32), (8, heads))]
    ).astype(bf16)
    all_gains = mm(gains, head_spread(heads, width, 0))
    row = iota((16, 256), 0)
    ends = jnp.where(row == 0, id_row, jnp.where(row == 3, id_row[:, :1], id_row[:, n_tok - 1 :]))

    total = jnp.zeros((n_tok, w.shape[1]), f32)
    for k in range(4):
        at = slice(chunk * k, chunk * k + chunk)
        parts[k][0].wait()
        parts[k][1].wait()
        total += mm(inp[:, at], w[at, :])
    proj = total.astype(bf16)
    proj_out[...] = proj
    proj_t = proj.astype(f32).T.astype(bf16)
    half = proj.shape[1] // 2
    b_t, c_t = proj_t[:half], proj_t[half:]
    for m in range(3):
        whole[2 + m].wait()
    sends = []
    for i in range(owners // 2):
        if i % 2 == 0:
            whole[5 + i].wait()
            whole[6 + i].wait()
        cols = slice(256 * i, 256 * i + 256)
        spread = head_spread(heads, 256, 4 * i)
        xs = (x[:, cols].astype(f32) * mm(to_end, spread)).astype(bf16)
        gs = (g[:, cols].astype(f32) * mm(from_start, spread)).astype(bf16)
        end_state = mm(b_t, xs).astype(bf16)
        start_grad = mm(c_t, gs).astype(bf16)
        gain_rows = all_gains[:, cols]
        for k in range(2):
            part = slice(128 * k, 128 * k + 128)
            buf[2 * i + k, 0:128, 0:128] = end_state[:, part]
            buf[2 * i + k, 0:128, 128:256] = start_grad[:, part]
            gain_hi_row = jnp.concatenate([gain_rows[0:1, part]] * 2, axis=1)
            gain_lo_row = jnp.concatenate([gain_rows[8:9, part]] * 2, axis=1)
            meta = jnp.where(row == 1, gain_hi_row, jnp.where(row == 2, gain_lo_row, ends))
            buf[2 * i + k, 128:144, :] = meta.astype(bf16)
        for m in range(3):
            block = qkv[m, :, 128 * i : 128 * i + 128].astype(f32)
            if m == 0:
                block = block * HEAD ** (-0.5)
            turned = block.T.astype(bf16)
            at = slice(144 + HEAD * m, 144 + HEAD * m + HEAD)
            buf[2 * i, at, :] = turned[:HEAD]
            buf[2 * i + 1, at, :] = turned[HEAD:]
        span = pl.ds(2 * i, 2)
        sends.append(pltpu.make_async_copy(buf.at[span], buf_hbm.at[span], out_sem.at[i]))
        sends[-1].start()
    for copy in sends:
        copy.wait()


def chain_kernel(recv, after, send):
    count = recv.shape[0]
    meta = [recv[k, 128:144, :].astype(f32) for k in range(count)]
    gain = [m[1:2, :128] + m[2:3, :128] for m in meta]
    link = [jnp.zeros((1, 128), f32)]
    for k in range(1, count):
        link.append(jnp.where(meta[k][3:4, :128] == meta[k - 1][4:5, :128], 1.0, 0.0))
    state = jnp.zeros((128, 128), f32)
    for k in range(count):
        state = state * link[k]
        send[k, :, 0:128] = state.astype(bf16)
        state = state * gain[k] + recv[k, 0:128, 0:128].astype(f32)
    adjoint = jnp.zeros((128, 128), f32)
    for k in range(count - 1, -1, -1):
        send[k, :, 128:256] = adjoint.astype(bf16)
        adjoint = (adjoint * gain[k] + recv[k, 0:128, 128:256].astype(f32)) * link[k]


def intra_kernel(inp, proj, x, g, te, fs, decay_t, ids, d_out, grad_out, kept, done, mixed):
    done[...] = jnp.zeros(done.shape, f32)
    n_tok = inp.shape[0]
    heads = decay_t.shape[0]
    half = proj.shape[1] // 2
    square = (n_tok, n_tok)
    early, late = iota(square, 0), iota(square, 1)
    run = mm_nt(ones_where(early >= late), decay_t[...])
    run_t = mm(decay_t[...], ones_where(early <= late))
    id_row = ids[...].astype(f32)
    id_col = id_column(id_row)[:, :1]
    bias = jnp.where((early <= late) & (id_col == id_row), 0.0, -1e30)
    b_rows, c_rows = proj[:, :half], proj[:, half:]
    b_dot_c = mm_nt(b_rows, c_rows)
    low_lane = iota((n_tok, 128), 1) < 64
    mixed[...] = jnp.zeros(square, f32)
    for p in range(heads // 2):
        cols = slice(128 * p, 128 * p + 128)
        xp, gp = x[:, cols], g[:, cols]
        zero = jnp.zeros_like(gp)
        total = jnp.zeros((n_tok, 128), f32)
        for k in range(2):
            h = 2 * p + k
            gh = jnp.where(low_lane, gp, zero) if k == 0 else jnp.where(low_lane, zero, gp)
            keep = jnp.exp(run_t[h : h + 1, :] - run[:, h : h + 1] + bias)
            mixed[...] += keep * mm_nt(xp, gh)
            total += mm((keep * b_dot_c).astype(bf16), gh)
        d_out[:, cols] = total
        spread = head_spread(heads, 128, 2 * p)
        rows = slice(n_tok * (p // 2), n_tok * (p // 2) + n_tok)
        side = slice(128 * (p % 2), 128 * (p % 2) + 128)
        kept[0, rows, side] = (xp.astype(f32) * mm(te[...], spread)).astype(bf16)
        kept[1, rows, side] = (gp.astype(f32) * mm(fs[...], spread)).astype(bf16)
        kept[2, cols, :] = inp[:, cols].astype(f32).T.astype(bf16)
    both = mixed[...]
    grad_out[:, :half] = mm(both.astype(bf16), c_rows)
    grad_out[:, half:] = mm(both.T.astype(bf16), b_rows)


def outer_kernel(core, recv_hbm, kept_hbm, grad_in, after, og_out, keep, give, recv, kept, sem):
    owners = recv.shape[0]
    n_tok = grad_in.shape[0]
    copies, arrivals = [], []
    for q in range(4):
        rows = pl.ds(kept.shape[1] // 4 * q, kept.shape[1] // 4)
        for k in range(2):
            copies.append(pltpu.make_async_copy(kept_hbm.at[k, rows], kept.at[k, rows], sem.at[2 * q + k]))
        span = pl.ds(owners // 4 * q, owners // 4)
        arrivals.append(pltpu.make_async_copy(recv_hbm.at[span], recv.at[span], sem.at[9 + q]))
        arrivals[-1].start()
        copies[2 * q].start()
        copies[2 * q + 1].start()
    copies.append(pltpu.make_async_copy(kept_hbm.at[2], kept.at[2], sem.at[8]))
    copies[8].start()
    grad_b = grad_in[:, :128]
    grad_c = grad_in[:, 128:]
    for i in range(owners // 2):
        if i % 2 == 0:
            copies[i].wait()
            copies[i + 1].wait()
            arrivals[i // 2].wait()
        rows = slice(n_tok * i, n_tok * i + n_tok)
        enter = jnp.concatenate([recv[2 * i, :, 0:128], recv[2 * i + 1, :, 0:128]], axis=1)
        leave = jnp.concatenate([recv[2 * i, :, 128:256], recv[2 * i + 1, :, 128:256]], axis=1)
        grad_b += mm_nt(kept[0, rows, :], leave)
        grad_c += mm_nt(kept[1, rows, :], enter)
    og_out[:, :128] = grad_b.astype(bf16)
    og_out[:, 128:] = grad_c.astype(bf16)
    og = og_out[...]
    copies[8].wait()
    rows = kept.shape[1] // owners // 2
    mine = pl.multiple_of(core[0] * rows, rows)
    other = pl.multiple_of(rows - core[0] * rows, rows)
    for first, out in ((mine, keep), (other, give)):
        half = jnp.concatenate([kept[2, pl.ds(2 * rows * j + first, rows), :] for j in range(owners)])
        out[...] = mm(half, og).astype(bf16).reshape(out.shape)


def input_grad_kernel(recv, proj, te, d_in, dx_out, done):
    done[...] = jnp.zeros(done.shape, f32)
    owners = recv.shape[0]
    heads = te.shape[1]
    b_rows = proj[:, : proj.shape[1] // 2]
    for i in range(owners // 2):
        cols = slice(256 * i, 256 * i + 256)
        leave = jnp.concatenate([recv[2 * i, :, 128:256], recv[2 * i + 1, :, 128:256]], axis=1)
        spread = mm(te[...], head_spread(heads, 256, 4 * i))
        dx_out[:, cols] = (d_in[:, cols] + spread * mm(b_rows, leave)).astype(bf16)


def attention_kernel(lows, qkv, out, done, keys, values):
    done[...] = jnp.zeros(done.shape, f32)
    blocks = qkv.shape[0]
    n = qkv.shape[2]
    slot = iota((16, n), 0).astype(f32)
    zeros48 = jnp.zeros((48, n), f32)

    def prepare(k, carry):
        ids = qkv[k, 128:144, :].astype(f32)[0:1]
        other = jnp.where(ids == slot, 0.0, -BIG)
        tall = jnp.concatenate([qkv[k, 208:272, :].astype(f32), other, zeros48])
        keys[pl.ds(pl.multiple_of(k * n, n), n), :] = tall.T.astype(bf16)
        values[k, 0:64, :] = qkv[k, 272:336, :]
        values[k, 64:80, :] = jnp.ones((16, n), bf16)
        return carry

    lax.fori_loop(0, blocks, prepare, 0)
    later = iota((2 * n, n), 0) - iota((2 * n, n), 1)
    masks = [jnp.where(later > k * n, -BIG, 0.0) for k in range(2)]

    def per_pair(c, carry):
        queries = []
        for k in range(2):
            ids = qkv[2 * c + k, 128:144, :].astype(f32)[0:1]
            own = jnp.where(ids == slot, 1.0, 0.0)
            rows = qkv[2 * c + k, 144:208, :].astype(f32)
            queries.append(jnp.concatenate([rows, own, zeros48]).astype(bf16))

        def scores(at, query):
            return mm(keys[pl.ds(pl.multiple_of(at * n, n), 2 * n), :], query)

        def weighted(at, p):
            return mm(values[at], p[:n]) + mm(values[at + 1], p[n:])

        held = []
        for k in range(2):
            s = scores(2 * c, queries[k]) + masks[k]
            top = jnp.max(s, axis=0, keepdims=True)
            held += [top, weighted(2 * c, jnp.exp(s - top).astype(bf16))]

        def step(i, held):
            at = 2 * (c - i)
            new = []
            s = [scores(at, query) for query in queries]
            for k in range(2):
                top, total = held[2 * k], held[2 * k + 1]
                new_top = jnp.maximum(top, jnp.max(s[k], axis=0, keepdims=True))
                p = jnp.exp(s[k] - new_top).astype(bf16)
                new += [new_top, total * jnp.exp(top - new_top) + weighted(at, p)]
            return tuple(new)

        held = lax.fori_loop(1, c + 1 - lows[2 * c] // 2, step, tuple(held))
        for k in range(2):
            total = held[2 * k + 1]
            out[2 * c + k] = (total[0:64] / total[64:65]).astype(bf16)
        return carry

    lax.fori_loop(0, blocks // 2, per_pair, 0)


def unpack_kernel(recv, out, done):
    done[...] = jnp.zeros(done.shape, f32)
    for i in range(recv.shape[0] // 2):
        tall = jnp.concatenate([recv[2 * i], recv[2 * i + 1]]).astype(f32)
        out[:, 128 * i : 128 * i + 128] = tall.T.astype(bf16)


def share_sum_kernel(recv, after, passed, out, passed_out):
    total = recv[0].astype(f32)
    for k in range(1, recv.shape[0]):
        total += recv[k].astype(f32)
    out[...] = total.astype(bf16)


def plane_sum_kernel(part, met, after, out):
    total = (part[...].astype(f32) + met[...].astype(f32)).astype(bf16)
    for k in range(out.shape[0]):
        out[k] = total


def assemble_kernel(core, mine, other, out, *, scale):
    for j in range(out.shape[0]):
        out[j, core[0]] = mine[j].astype(f32) * scale
        out[j, 1 - core[0]] = other[j].astype(f32) * scale


def exchange(blocks, axis):
    return lax.all_to_all(blocks, axis, split_axis=0, concat_axis=0, tiled=True)


def per_device(layer_input, proj_weight, ssd_input, log_decay, segment_ids, ssd_cotangent, window_qkv):
    inp, x, g = layer_input[0], ssd_input[0], ssd_cotangent[0]
    decay_t = log_decay[0].T
    qkv = window_qkv[0].transpose(1, 0, 2)
    n_tok, width = inp.shape
    heads = decay_t.shape[0]
    ctx = lax.axis_size("ctx")
    dp = lax.axis_size("dp")
    n_out = proj_weight.shape[1]
    core = lax.axis_index("dp") % 2
    pairs = [(i, i ^ 1) for i in range(dp)]

    done = sds((8, 128), f32)

    vmem = pl.BlockSpec(memory_space=pltpu.VMEM)
    anywhere = pl.BlockSpec(memory_space=pltpu.HBM)
    buf, proj, te, fs = pl.pallas_call(
        front_kernel,
        out_shape=(
            sds((ctx, 336, n_tok), bf16),
            sds((n_tok, n_out), bf16),
            sds((n_tok, heads), bf16),
            sds((n_tok, heads), bf16),
        ),
        in_specs=[anywhere] * 7,
        out_specs=(anywhere, vmem, vmem, vmem),
        scratch_shapes=[
            pltpu.VMEM(a.shape, a.dtype) for a in (inp, proj_weight, x, g, qkv, decay_t, segment_ids)
        ]
        + [
            pltpu.VMEM((ctx, 336, n_tok), bf16),
            pltpu.SemaphoreType.DMA((13,)),
            pltpu.SemaphoreType.DMA((2, 4)),
            pltpu.SemaphoreType.DMA((ctx // 2,)),
        ],
        compiler_params=pltpu.CompilerParams(vmem_limit_bytes=64 << 20),
        cost_estimate=pl.CostEstimate(flops=2 << 30, bytes_accessed=9 << 20, transcendentals=0),
    )(inp, proj_weight, x, g, qkv, decay_t, segment_ids)
    got = exchange(buf, "ctx")

    d_intra, grad_intra, kept, intra_done = call(
        intra_kernel,
        (
            sds((n_tok, width), f32),
            sds((n_tok, n_out), f32),
            sds((3, width, n_tok), bf16),
            done,
        ),
        inp, proj, x, g, te, fs, decay_t, segment_ids,
        scratch=[pltpu.VMEM((n_tok, n_tok), f32)],
        flops=6 << 30, n_bytes=8 << 20,
    )
    sent = call(
        chain_kernel,
        sds((ctx, 128, 256), bf16),
        got, intra_done,
        n_bytes=6 << 20,
    )
    back = exchange(sent, "ctx")

    ids = got[:, 128, :].astype(jnp.int32)
    lows = jnp.sum(ids[None, :, -1] < ids[:, None, 0], axis=1, dtype=jnp.int32)
    attended, attention_done = call(
        attention_kernel,
        (sds((ctx, HEAD, n_tok), bf16), done),
        lows, got,
        scratch=[pltpu.VMEM((ctx * n_tok, 128), bf16), pltpu.VMEM((ctx, 80, n_tok), bf16)],
        flops=16 << 30, n_bytes=2 << 20, prefetch=1,
    )

    half_rows = width // ctx // 2
    out_grad, keep, give = call(
        outer_kernel,
        (sds((n_tok, n_out), bf16), sds((ctx, half_rows, n_out), bf16), sds((ctx, half_rows, n_out), bf16)),
        core[None], back, kept, grad_intra, attention_done,
        scratch=[
            pltpu.VMEM((ctx, 128, 256), bf16),
            pltpu.VMEM((3, width, n_tok), bf16),
            pltpu.SemaphoreType.DMA((13,)),
        ],
        flops=2 << 30, n_bytes=6 << 20, prefetch=1, limit=61 << 20, hbm=(1, 2),
    )
    given = lax.ppermute(give, "dp", pairs)
    share = (keep.astype(f32) + given.astype(f32)).astype(bf16)
    shares = exchange(share, "ctx")
    input_grad, input_done = call(
        input_grad_kernel,
        (sds((n_tok, width), bf16), done),
        back, proj, te, d_intra,
        flops=1 << 30, n_bytes=4 << 20,
    )
    part, attended = pl.pallas_call(
        share_sum_kernel,
        out_shape=(sds((half_rows, n_out), bf16), sds(attended.shape, bf16)),
        in_specs=[vmem, vmem, anywhere],
        out_specs=(vmem, anywhere),
        input_output_aliases={2: 1},
        compiler_params=pltpu.CompilerParams(vmem_limit_bytes=24 << 20),
        cost_estimate=pl.CostEstimate(flops=0, bytes_accessed=1 << 20, transcendentals=0),
    )(shares, input_done, attended)
    out_rows = exchange(attended, "ctx")
    window_out, window_done = call(
        unpack_kernel, (sds((n_tok, ctx * HEAD), bf16), done), out_rows, n_bytes=1 << 20
    )
    step = 2
    while 2 * step < dp:
        met = lax.ppermute(part, "dp", [(i, i ^ step) for i in range(dp)])
        part = (part.astype(f32) + met.astype(f32)).astype(bf16)
        step *= 2
    met = lax.ppermute(part, "dp", [(i, i ^ step) for i in range(dp)])
    strip = call(plane_sum_kernel, sds((ctx, half_rows, n_out), bf16), part, met, window_done, n_bytes=1 << 20)
    mine = exchange(strip, "ctx")
    other = lax.ppermute(mine, "dp", pairs)
    weight_grad = call(
        functools.partial(assemble_kernel, scale=1.0 / math.sqrt(dp * ctx * n_tok)),
        sds((ctx, 2, half_rows, n_out), f32),
        core[None], mine, other,
        n_bytes=4 << 20, prefetch=1,
    ).reshape(width, n_out)
    return (input_grad[None], out_grad[None], weight_grad, window_out[None])


def solution(mesh):
    placed = (
        P("dp", "ctx", None),
        P(),
        P("dp", "ctx", None),
        P("dp", "ctx", None),
        P("dp", "ctx"),
        P("dp", "ctx", None),
        P("dp", "ctx", None, None),
    )
    return jax.shard_map(
        per_device,
        mesh=mesh,
        in_specs=placed,
        out_specs=(P("dp", "ctx", None), P("dp", "ctx", None), P(), P("dp", "ctx", None)),
        check_vma=False,
    )
```

```python
import functools
import math

import jax
import jax.numpy as jnp
from jax import lax
from jax.experimental import pallas as pl
from jax.experimental.pallas import tpu as pltpu
from jax.sharding import PartitionSpec as P

HEAD = 64
BIG = 16384.0
f32 = jnp.float32
bf16 = jnp.bfloat16
NT = (((1,), (1,)), ((), ()))


def mm(a, b):
    return jnp.dot(a, b, preferred_element_type=f32)


def mm_nt(a, b):
    return lax.dot_general(a, b, NT, preferred_element_type=f32)


def iota(shape, dim):
    return lax.broadcasted_iota(jnp.int32, shape, dim)


def ones_where(cond):
    return jnp.where(cond, 1.0, 0.0).astype(bf16)


def head_spread(heads, width, first):
    return ones_where(iota((heads, width), 0) == (iota((heads, width), 1) >> 6) + first)


def id_column(id_row):
    n = id_row.shape[1]
    eye = ones_where(iota((n, n), 0) == iota((n, n), 1))
    return mm_nt(eye, jnp.broadcast_to(id_row, (128, n)).astype(bf16))


def call(kernel, out_shape, *args, scratch=(), flops=0, n_bytes=4 << 20, prefetch=0, limit=24 << 20, hbm=()):
    vmem = pl.BlockSpec(memory_space=pltpu.VMEM)
    smem = pl.BlockSpec(memory_space=pltpu.SMEM)
    any_hbm = pl.BlockSpec(memory_space=pltpu.HBM)
    many = isinstance(out_shape, (list, tuple))
    return pl.pallas_call(
        kernel,
        out_shape=out_shape,
        in_specs=[smem if k < prefetch else any_hbm if k in hbm else vmem for k in range(len(args))],
        out_specs=[vmem] * len(out_shape) if many else vmem,
        scratch_shapes=list(scratch),
        compiler_params=pltpu.CompilerParams(vmem_limit_bytes=limit),
        cost_estimate=pl.CostEstimate(flops=flops, bytes_accessed=n_bytes, transcendentals=0),
    )(*args)


def sds(shape, dtype):
    return jax.ShapeDtypeStruct(shape, dtype)


def front_kernel(
    inp_hbm, w_hbm, x_hbm, g_hbm, qkv_hbm, decay_hbm, ids_hbm,
    buf_hbm, proj_out, te_out, fs_out,
    inp, w, x, g, qkv, decay_t, ids, buf, in_sem, part_sem, out_sem,
):
    n_tok, width = inp.shape
    heads = decay_t.shape[0]
    owners = buf.shape[0]
    whole = [
        pltpu.make_async_copy(src, dst, in_sem.at[k])
        for k, (src, dst) in enumerate(
            [(decay_hbm, decay_t), (ids_hbm, ids)]
            + [(qkv_hbm.at[m], qkv.at[m]) for m in range(3)]
            + [
                (src.at[:, pl.ds(width // 4 * q, width // 4)], dst.at[:, pl.ds(width // 4 * q, width // 4)])
                for q in range(4)
                for src, dst in ((x_hbm, x), (g_hbm, g))
            ]
        )
    ]
    chunk = width // 4
    parts = []
    for k in range(4):
        at = pl.ds(chunk * k, chunk)
        parts.append(
            (
                pltpu.make_async_copy(inp_hbm.at[:, at], inp.at[:, at], part_sem.at[0, k]),
                pltpu.make_async_copy(w_hbm.at[at, :], w.at[at, :], part_sem.at[1, k]),
            )
        )
    whole[0].start()
    whole[1].start()
    for pair in parts:
        pair[0].start()
        pair[1].start()
    for copy in whole[5:] + whole[2:5]:
        copy.start()

    early, late = iota((n_tok, n_tok), 0), iota((n_tok, n_tok), 1)
    tri = ones_where(early >= late)
    whole[0].wait()
    whole[1].wait()
    run = mm_nt(tri, decay_t[...])
    final = run[n_tok - 1 : n_tok]
    id_row = ids[...].astype(f32)
    id_col = id_column(id_row)[:, :heads]
    first, last = id_col[:1], id_col[n_tok - 1 :]
    to_end = jnp.where(id_col == last, jnp.exp(final - run), 0.0).astype(bf16)
    from_start = jnp.where(id_col == first, jnp.exp(run), 0.0).astype(bf16)
    te_out[...] = to_end
    fs_out[...] = from_start
    gain = jnp.where(first == last, jnp.exp(final), 0.0)
    gain_hi = gain.astype(bf16)
    gain_lo = (gain - gain_hi.astype(f32)).astype(bf16)
    gains = jnp.concatenate(
        [jnp.broadcast_to(gain_hi.astype(f32), (8, heads)), jnp.broadcast_to(gain_lo.astype(f32), (8, heads))]
    ).astype(bf16)
    all_gains = mm(gains, head_spread(heads, width, 0))
    row = iota((16, 256), 0)
    ends = jnp.where(row == 0, id_row, jnp.where(row == 3, id_row[:, :1], id_row[:, n_tok - 1 :]))

    total = jnp.zeros((n_tok, w.shape[1]), f32)
    for k in range(4):
        at = slice(chunk * k, chunk * k + chunk)
        parts[k][0].wait()
        parts[k][1].wait()
        total += mm(inp[:, at], w[at, :])
    proj = total.astype(bf16)
    proj_out[...] = proj
    proj_t = proj.astype(f32).T.astype(bf16)
    half = proj.shape[1] // 2
    b_t, c_t = proj_t[:half], proj_t[half:]
    for m in range(3):
        whole[2 + m].wait()
    sends = []
    for i in range(owners // 2):
        if i % 2 == 0:
            whole[5 + i].wait()
            whole[6 + i].wait()
        cols = slice(256 * i, 256 * i + 256)
        spread = head_spread(heads, 256, 4 * i)
        xs = (x[:, cols].astype(f32) * mm(to_end, spread)).astype(bf16)
        gs = (g[:, cols].astype(f32) * mm(from_start, spread)).astype(bf16)
        end_state = mm(b_t, xs).astype(bf16)
        start_grad = mm(c_t, gs).astype(bf16)
        gain_rows = all_gains[:, cols]
        for k in range(2):
            part = slice(128 * k, 128 * k + 128)
            buf[2 * i + k, 0:128, 0:128] = end_state[:, part]
            buf[2 * i + k, 0:128, 128:256] = start_grad[:, part]
            gain_hi_row = jnp.concatenate([gain_rows[0:1, part]] * 2, axis=1)
            gain_lo_row = jnp.concatenate([gain_rows[8:9, part]] * 2, axis=1)
            meta = jnp.where(row == 1, gain_hi_row, jnp.where(row == 2, gain_lo_row, ends))
            buf[2 * i + k, 128:144, :] = meta.astype(bf16)
        for m in range(3):
            block = qkv[m, :, 128 * i : 128 * i + 128].astype(f32)
            if m == 0:
                block = block * HEAD ** (-0.5)
            turned = block.T.astype(bf16)
            at = slice(144 + HEAD * m, 144 + HEAD * m + HEAD)
            buf[2 * i, at, :] = turned[:HEAD]
            buf[2 * i + 1, at, :] = turned[HEAD:]
        span = pl.ds(2 * i, 2)
        sends.append(pltpu.make_async_copy(buf.at[span], buf_hbm.at[span], out_sem.at[i]))
        sends[-1].start()
    for copy in sends:
        copy.wait()


def chain_kernel(recv, after, send):
    count = recv.shape[0]
    meta = [recv[k, 128:144, :].astype(f32) for k in range(count)]
    gain = [m[1:2, :128] + m[2:3, :128] for m in meta]
    link = [jnp.zeros((1, 128), f32)]
    for k in range(1, count):
        link.append(jnp.where(meta[k][3:4, :128] == meta[k - 1][4:5, :128], 1.0, 0.0))
    state = jnp.zeros((128, 128), f32)
    for k in range(count):
        state = state * link[k]
        send[k, :, 0:128] = state.astype(bf16)
        state = state * gain[k] + recv[k, 0:128, 0:128].astype(f32)
    adjoint = jnp.zeros((128, 128), f32)
    for k in range(count - 1, -1, -1):
        send[k, :, 128:256] = adjoint.astype(bf16)
        adjoint = (adjoint * gain[k] + recv[k, 0:128, 128:256].astype(f32)) * link[k]


def intra_kernel(inp, proj, x, g, te, fs, decay_t, ids, d_out, grad_out, kept, done, mixed):
    done[...] = jnp.zeros(done.shape, f32)
    n_tok = inp.shape[0]
    heads = decay_t.shape[0]
    half = proj.shape[1] // 2
    square = (n_tok, n_tok)
    early, late = iota(square, 0), iota(square, 1)
    run = mm_nt(ones_where(early >= late), decay_t[...])
    run_t = mm(decay_t[...], ones_where(early <= late))
    id_row = ids[...].astype(f32)
    id_col = id_column(id_row)[:, :1]
    bias = jnp.where((early <= late) & (id_col == id_row), 0.0, -1e30)
    b_rows, c_rows = proj[:, :half], proj[:, half:]
    b_dot_c = mm_nt(b_rows, c_rows)
    low_lane = iota((n_tok, 128), 1) < 64
    mixed[...] = jnp.zeros(square, f32)
    for p in range(heads // 2):
        cols = slice(128 * p, 128 * p + 128)
        xp, gp = x[:, cols], g[:, cols]
        zero = jnp.zeros_like(gp)
        total = jnp.zeros((n_tok, 128), f32)
        for k in range(2):
            h = 2 * p + k
            gh = jnp.where(low_lane, gp, zero) if k == 0 else jnp.where(low_lane, zero, gp)
            keep = jnp.exp(run_t[h : h + 1, :] - run[:, h : h + 1] + bias)
            mixed[...] += keep * mm_nt(xp, gh)
            total += mm((keep * b_dot_c).astype(bf16), gh)
        d_out[:, cols] = total
        spread = head_spread(heads, 128, 2 * p)
        rows = slice(n_tok * (p // 2), n_tok * (p // 2) + n_tok)
        side = slice(128 * (p % 2), 128 * (p % 2) + 128)
        kept[0, rows, side] = (xp.astype(f32) * mm(te[...], spread)).astype(bf16)
        kept[1, rows, side] = (gp.astype(f32) * mm(fs[...], spread)).astype(bf16)
        kept[2, cols, :] = inp[:, cols].astype(f32).T.astype(bf16)
    both = mixed[...]
    grad_out[:, :half] = mm(both.astype(bf16), c_rows)
    grad_out[:, half:] = mm(both.T.astype(bf16), b_rows)


def outer_kernel(core, recv_hbm, kept_hbm, grad_in, after, og_out, keep, give, recv, kept, sem):
    owners = recv.shape[0]
    n_tok = grad_in.shape[0]
    copies, arrivals = [], []
    for q in range(4):
        rows = pl.ds(kept.shape[1] // 4 * q, kept.shape[1] // 4)
        for k in range(2):
            copies.append(pltpu.make_async_copy(kept_hbm.at[k, rows], kept.at[k, rows], sem.at[2 * q + k]))
        span = pl.ds(owners // 4 * q, owners // 4)
        arrivals.append(pltpu.make_async_copy(recv_hbm.at[span], recv.at[span], sem.at[9 + q]))
        arrivals[-1].start()
        copies[2 * q].start()
        copies[2 * q + 1].start()
    copies.append(pltpu.make_async_copy(kept_hbm.at[2], kept.at[2], sem.at[8]))
    copies[8].start()
    grad_b = grad_in[:, :128]
    grad_c = grad_in[:, 128:]
    for i in range(owners // 2):
        if i % 2 == 0:
            copies[i].wait()
            copies[i + 1].wait()
            arrivals[i // 2].wait()
        rows = slice(n_tok * i, n_tok * i + n_tok)
        enter = jnp.concatenate([recv[2 * i, :, 0:128], recv[2 * i + 1, :, 0:128]], axis=1)
        leave = jnp.concatenate([recv[2 * i, :, 128:256], recv[2 * i + 1, :, 128:256]], axis=1)
        grad_b += mm_nt(kept[0, rows, :], leave)
        grad_c += mm_nt(kept[1, rows, :], enter)
    og_out[:, :128] = grad_b.astype(bf16)
    og_out[:, 128:] = grad_c.astype(bf16)
    og = og_out[...]
    copies[8].wait()
    rows = kept.shape[1] // owners // 2
    mine = pl.multiple_of(core[0] * rows, rows)
    other = pl.multiple_of(rows - core[0] * rows, rows)
    for first, out in ((mine, keep), (other, give)):
        half = jnp.concatenate([kept[2, pl.ds(2 * rows * j + first, rows), :] for j in range(owners)])
        out[...] = mm(half, og).astype(bf16).reshape(out.shape)


def input_grad_kernel(recv, proj, te, d_in, after, dx_out, done):
    done[...] = jnp.zeros(done.shape, f32)
    owners = recv.shape[0]
    heads = te.shape[1]
    b_rows = proj[:, : proj.shape[1] // 2]
    for i in range(owners // 2):
        cols = slice(256 * i, 256 * i + 256)
        leave = jnp.concatenate([recv[2 * i, :, 128:256], recv[2 * i + 1, :, 128:256]], axis=1)
        spread = mm(te[...], head_spread(heads, 256, 4 * i))
        dx_out[:, cols] = (d_in[:, cols] + spread * mm(b_rows, leave)).astype(bf16)


def attention_kernel(lows, qkv, after, out, done, keys, values, *, begin):
    done[...] = jnp.zeros(done.shape, f32)
    blocks = begin + out.shape[0]
    n = qkv.shape[2]
    slot = iota((16, n), 0).astype(f32)
    zeros48 = jnp.zeros((48, n), f32)

    def prepare(k, carry):
        ids = qkv[k, 128:144, :].astype(f32)[0:1]
        other = jnp.where(ids == slot, 0.0, -BIG)
        tall = jnp.concatenate([qkv[k, 208:272, :].astype(f32), other, zeros48])
        keys[pl.ds(pl.multiple_of(k * n, n), n), :] = tall.T.astype(bf16)
        values[k, 0:64, :] = qkv[k, 272:336, :]
        values[k, 64:80, :] = jnp.ones((16, n), bf16)
        return carry

    lax.fori_loop(lows[begin] // 2 * 2, blocks, prepare, 0)
    later = iota((2 * n, n), 0) - iota((2 * n, n), 1)
    masks = [jnp.where(later > k * n, -BIG, 0.0) for k in range(2)]

    def per_pair(c, carry):
        queries = []
        for k in range(2):
            ids = qkv[2 * c + k, 128:144, :].astype(f32)[0:1]
            own = jnp.where(ids == slot, 1.0, 0.0)
            rows = qkv[2 * c + k, 144:208, :].astype(f32)
            queries.append(jnp.concatenate([rows, own, zeros48]).astype(bf16))

        def scores(at, query):
            return mm(keys[pl.ds(pl.multiple_of(at * n, n), 2 * n), :], query)

        def weighted(at, p):
            return mm(values[at], p[:n]) + mm(values[at + 1], p[n:])

        held = []
        for k in range(2):
            s = scores(2 * c, queries[k]) + masks[k]
            top = jnp.max(s, axis=0, keepdims=True)
            held += [top, weighted(2 * c, jnp.exp(s - top).astype(bf16))]

        def step(i, held):
            at = 2 * (c - i)
            new = []
            s = [scores(at, query) for query in queries]
            for k in range(2):
                top, total = held[2 * k], held[2 * k + 1]
                new_top = jnp.maximum(top, jnp.max(s[k], axis=0, keepdims=True))
                p = jnp.exp(s[k] - new_top).astype(bf16)
                new += [new_top, total * jnp.exp(top - new_top) + weighted(at, p)]
            return tuple(new)

        held = lax.fori_loop(1, c + 1 - lows[2 * c] // 2, step, tuple(held))
        for k in range(2):
            total = held[2 * k + 1]
            out[2 * c + k - begin] = (total[0:64] / total[64:65]).astype(bf16)
        return carry

    lax.fori_loop(begin // 2, blocks // 2, per_pair, 0)


def unpack_kernel(recv, out, done):
    done[...] = jnp.zeros(done.shape, f32)
    for i in range(recv.shape[0] // 2):
        tall = jnp.concatenate([recv[2 * i], recv[2 * i + 1]]).astype(f32)
        out[:, 128 * i : 128 * i + 128] = tall.T.astype(bf16)


def share_sum_kernel(recv, after, passed, out, passed_out):
    total = recv[0].astype(f32)
    for k in range(1, recv.shape[0]):
        total += recv[k].astype(f32)
    out[...] = total.astype(bf16)


def plane_sum_kernel(part, met, after, out):
    total = (part[...].astype(f32) + met[...].astype(f32)).astype(bf16)
    for k in range(out.shape[0]):
        out[k] = total


def assemble_kernel(core, mine, other, out, *, scale):
    for j in range(out.shape[0]):
        out[j, core[0]] = mine[j].astype(f32) * scale
        out[j, 1 - core[0]] = other[j].astype(f32) * scale


def exchange(blocks, axis):
    return lax.all_to_all(blocks, axis, split_axis=0, concat_axis=0, tiled=True)


def per_device(layer_input, proj_weight, ssd_input, log_decay, segment_ids, ssd_cotangent, window_qkv):
    inp, x, g = layer_input[0], ssd_input[0], ssd_cotangent[0]
    decay_t = log_decay[0].T
    qkv = window_qkv[0].transpose(1, 0, 2)
    n_tok, width = inp.shape
    heads = decay_t.shape[0]
    ctx = lax.axis_size("ctx")
    dp = lax.axis_size("dp")
    n_out = proj_weight.shape[1]
    core = lax.axis_index("dp") % 2
    pairs = [(i, i ^ 1) for i in range(dp)]

    done = sds((8, 128), f32)

    vmem = pl.BlockSpec(memory_space=pltpu.VMEM)
    anywhere = pl.BlockSpec(memory_space=pltpu.HBM)
    buf, proj, te, fs = pl.pallas_call(
        front_kernel,
        out_shape=(
            sds((ctx, 336, n_tok), bf16),
            sds((n_tok, n_out), bf16),
            sds((n_tok, heads), bf16),
            sds((n_tok, heads), bf16),
        ),
        in_specs=[anywhere] * 7,
        out_specs=(anywhere, vmem, vmem, vmem),
        scratch_shapes=[
            pltpu.VMEM(a.shape, a.dtype) for a in (inp, proj_weight, x, g, qkv, decay_t, segment_ids)
        ]
        + [
            pltpu.VMEM((ctx, 336, n_tok), bf16),
            pltpu.SemaphoreType.DMA((13,)),
            pltpu.SemaphoreType.DMA((2, 4)),
            pltpu.SemaphoreType.DMA((ctx // 2,)),
        ],
        compiler_params=pltpu.CompilerParams(vmem_limit_bytes=64 << 20),
        cost_estimate=pl.CostEstimate(flops=2 << 30, bytes_accessed=9 << 20, transcendentals=0),
    )(inp, proj_weight, x, g, qkv, decay_t, segment_ids)
    got = exchange(buf, "ctx")

    d_intra, grad_intra, kept, intra_done = call(
        intra_kernel,
        (
            sds((n_tok, width), f32),
            sds((n_tok, n_out), f32),
            sds((3, width, n_tok), bf16),
            done,
        ),
        inp, proj, x, g, te, fs, decay_t, segment_ids,
        scratch=[pltpu.VMEM((n_tok, n_tok), f32)],
        flops=6 << 30, n_bytes=8 << 20,
    )
    sent = call(
        chain_kernel,
        sds((ctx, 128, 256), bf16),
        got, intra_done,
        n_bytes=6 << 20,
    )
    back = exchange(sent, "ctx")

    ids = got[:, 128, :].astype(jnp.int32)
    lows = jnp.sum(ids[None, :, -1] < ids[:, None, 0], axis=1, dtype=jnp.int32)
    def attend(begin, end, after):
        return call(
            functools.partial(attention_kernel, begin=begin),
            (sds((end - begin, HEAD, n_tok), bf16), done),
            lows, got, after,
            scratch=[pltpu.VMEM((end * n_tok, 128), bf16), pltpu.VMEM((end, 80, n_tok), bf16)],
            flops=8 << 30, n_bytes=2 << 20, prefetch=1, hbm=(2,),
        )

    split = ctx * 5 // 16 * 2
    attended, attention_done = attend(0, split, lows)

    half_rows = width // ctx // 2
    out_grad, keep, give = call(
        outer_kernel,
        (sds((n_tok, n_out), bf16), sds((ctx, half_rows, n_out), bf16), sds((ctx, half_rows, n_out), bf16)),
        core[None], back, kept, grad_intra, attention_done,
        scratch=[
            pltpu.VMEM((ctx, 128, 256), bf16),
            pltpu.VMEM((3, width, n_tok), bf16),
            pltpu.SemaphoreType.DMA((13,)),
        ],
        flops=2 << 30, n_bytes=6 << 20, prefetch=1, limit=61 << 20, hbm=(1, 2),
    )
    given = lax.ppermute(give, "dp", pairs)
    share = (keep.astype(f32) + given.astype(f32)).astype(bf16)
    shares = exchange(share, "ctx")
    attended = jnp.concatenate([attended, attend(split, ctx, share)[0]])
    input_grad, input_done = call(
        input_grad_kernel,
        (sds((n_tok, width), bf16), done),
        back, proj, te, d_intra, share,
        flops=1 << 30, n_bytes=4 << 20, hbm=(4,),
    )
    part, attended = pl.pallas_call(
        share_sum_kernel,
        out_shape=(sds((half_rows, n_out), bf16), sds(attended.shape, bf16)),
        in_specs=[vmem, vmem, anywhere],
        out_specs=(vmem, anywhere),
        input_output_aliases={2: 1},
        compiler_params=pltpu.CompilerParams(vmem_limit_bytes=24 << 20),
        cost_estimate=pl.CostEstimate(flops=0, bytes_accessed=1 << 20, transcendentals=0),
    )(shares, input_done, attended)
    out_rows = exchange(attended, "ctx")
    window_out, window_done = call(
        unpack_kernel, (sds((n_tok, ctx * HEAD), bf16), done), out_rows, n_bytes=1 << 20
    )
    step = 2
    while 2 * step < dp:
        met = lax.ppermute(part, "dp", [(i, i ^ step) for i in range(dp)])
        part = (part.astype(f32) + met.astype(f32)).astype(bf16)
        step *= 2
    met = lax.ppermute(part, "dp", [(i, i ^ step) for i in range(dp)])
    strip = call(plane_sum_kernel, sds((ctx, half_rows, n_out), bf16), part, met, window_done, n_bytes=1 << 20)
    mine = exchange(strip, "ctx")
    other = lax.ppermute(mine, "dp", pairs)
    weight_grad = call(
        functools.partial(assemble_kernel, scale=1.0 / math.sqrt(dp * ctx * n_tok)),
        sds((ctx, 2, half_rows, n_out), f32),
        core[None], mine, other,
        n_bytes=4 << 20, prefetch=1,
    ).reshape(width, n_out)
    return (input_grad[None], out_grad[None], weight_grad, window_out[None])


def solution(mesh):
    placed = (
        P("dp", "ctx", None),
        P(),
        P("dp", "ctx", None),
        P("dp", "ctx", None),
        P("dp", "ctx"),
        P("dp", "ctx", None),
        P("dp", "ctx", None, None),
    )
    return jax.shard_map(
        per_device,
        mesh=mesh,
        in_specs=placed,
        out_specs=(P("dp", "ctx", None), P("dp", "ctx", None), P(), P("dp", "ctx", None)),
        check_vma=False,
    )
```

```python
import functools
import math

import jax
import jax.numpy as jnp
from jax import lax
from jax.experimental import pallas as pl
from jax.experimental.pallas import tpu as pltpu
from jax.sharding import PartitionSpec as P

HEAD = 64
BIG = 16384.0
f32 = jnp.float32
bf16 = jnp.bfloat16
NT = (((1,), (1,)), ((), ()))


def mm(a, b):
    return jnp.dot(a, b, preferred_element_type=f32)


def mm_nt(a, b):
    return lax.dot_general(a, b, NT, preferred_element_type=f32)


def iota(shape, dim):
    return lax.broadcasted_iota(jnp.int32, shape, dim)


def ones_where(cond):
    return jnp.where(cond, 1.0, 0.0).astype(bf16)


def head_spread(heads, width, first):
    return ones_where(iota((heads, width), 0) == (iota((heads, width), 1) >> 6) + first)


def id_column(id_row):
    n = id_row.shape[1]
    eye = ones_where(iota((n, n), 0) == iota((n, n), 1))
    return mm_nt(eye, jnp.broadcast_to(id_row, (128, n)).astype(bf16))


def call(kernel, out_shape, *args, scratch=(), flops=0, n_bytes=4 << 20, prefetch=0, limit=24 << 20, hbm=()):
    vmem = pl.BlockSpec(memory_space=pltpu.VMEM)
    smem = pl.BlockSpec(memory_space=pltpu.SMEM)
    any_hbm = pl.BlockSpec(memory_space=pltpu.HBM)
    many = isinstance(out_shape, (list, tuple))
    return pl.pallas_call(
        kernel,
        out_shape=out_shape,
        in_specs=[smem if k < prefetch else any_hbm if k in hbm else vmem for k in range(len(args))],
        out_specs=[vmem] * len(out_shape) if many else vmem,
        scratch_shapes=list(scratch),
        compiler_params=pltpu.CompilerParams(vmem_limit_bytes=limit),
        cost_estimate=pl.CostEstimate(flops=flops, bytes_accessed=n_bytes, transcendentals=0),
    )(*args)


def sds(shape, dtype):
    return jax.ShapeDtypeStruct(shape, dtype)


def front_kernel(
    inp_hbm, w_hbm, x_hbm, g_hbm, qkv_hbm, decay_hbm, ids_hbm,
    buf_hbm, proj_out, te_out, fs_out,
    inp, w, x, g, qkv, decay_t, ids, buf, in_sem, part_sem, out_sem,
):
    n_tok, width = inp.shape
    heads = decay_t.shape[0]
    owners = buf.shape[0]
    whole = [
        pltpu.make_async_copy(src, dst, in_sem.at[k])
        for k, (src, dst) in enumerate(
            [(decay_hbm, decay_t), (ids_hbm, ids)]
            + [(qkv_hbm.at[m], qkv.at[m]) for m in range(3)]
            + [
                (src.at[:, pl.ds(width // 4 * q, width // 4)], dst.at[:, pl.ds(width // 4 * q, width // 4)])
                for q in range(4)
                for src, dst in ((x_hbm, x), (g_hbm, g))
            ]
        )
    ]
    chunk = width // 4
    parts = []
    for k in range(4):
        at = pl.ds(chunk * k, chunk)
        parts.append(
            (
                pltpu.make_async_copy(inp_hbm.at[:, at], inp.at[:, at], part_sem.at[0, k]),
                pltpu.make_async_copy(w_hbm.at[at, :], w.at[at, :], part_sem.at[1, k]),
            )
        )
    whole[0].start()
    whole[1].start()
    for pair in parts:
        pair[0].start()
        pair[1].start()
    for copy in whole[5:] + whole[2:5]:
        copy.start()

    early, late = iota((n_tok, n_tok), 0), iota((n_tok, n_tok), 1)
    tri = ones_where(early >= late)
    whole[0].wait()
    whole[1].wait()
    run = mm_nt(tri, decay_t[...])
    final = run[n_tok - 1 : n_tok]
    id_row = ids[...].astype(f32)
    id_col = id_column(id_row)[:, :heads]
    first, last = id_col[:1], id_col[n_tok - 1 :]
    to_end = jnp.where(id_col == last, jnp.exp(final - run), 0.0).astype(bf16)
    from_start = jnp.where(id_col == first, jnp.exp(run), 0.0).astype(bf16)
    te_out[...] = to_end
    fs_out[...] = from_start
    gain = jnp.where(first == last, jnp.exp(final), 0.0)
    gain_hi = gain.astype(bf16)
    gain_lo = (gain - gain_hi.astype(f32)).astype(bf16)
    gains = jnp.concatenate(
        [jnp.broadcast_to(gain_hi.astype(f32), (8, heads)), jnp.broadcast_to(gain_lo.astype(f32), (8, heads))]
    ).astype(bf16)
    all_gains = mm(gains, head_spread(heads, width, 0))
    row = iota((16, 256), 0)
    ends = jnp.where(row == 0, id_row, jnp.where(row == 3, id_row[:, :1], id_row[:, n_tok - 1 :]))

    total = jnp.zeros((n_tok, w.shape[1]), f32)
    for k in range(4):
        at = slice(chunk * k, chunk * k + chunk)
        parts[k][0].wait()
        parts[k][1].wait()
        total += mm(inp[:, at], w[at, :])
    proj = total.astype(bf16)
    proj_out[...] = proj
    proj_t = proj.astype(f32).T.astype(bf16)
    half = proj.shape[1] // 2
    b_t, c_t = proj_t[:half], proj_t[half:]
    for m in range(3):
        whole[2 + m].wait()
    sends = []
    for i in range(owners // 2):
        if i % 2 == 0:
            whole[5 + i].wait()
            whole[6 + i].wait()
        cols = slice(256 * i, 256 * i + 256)
        spread = head_spread(heads, 256, 4 * i)
        xs = (x[:, cols].astype(f32) * mm(to_end, spread)).astype(bf16)
        gs = (g[:, cols].astype(f32) * mm(from_start, spread)).astype(bf16)
        end_state = mm(b_t, xs).astype(bf16)
        start_grad = mm(c_t, gs).astype(bf16)
        gain_rows = all_gains[:, cols]
        for k in range(2):
            part = slice(128 * k, 128 * k + 128)
            buf[2 * i + k, 0:128, 0:128] = end_state[:, part]
            buf[2 * i + k, 0:128, 128:256] = start_grad[:, part]
            gain_hi_row = jnp.concatenate([gain_rows[0:1, part]] * 2, axis=1)
            gain_lo_row = jnp.concatenate([gain_rows[8:9, part]] * 2, axis=1)
            meta = jnp.where(row == 1, gain_hi_row, jnp.where(row == 2, gain_lo_row, ends))
            buf[2 * i + k, 128:144, :] = meta.astype(bf16)
        for m in range(3):
            block = qkv[m, :, 128 * i : 128 * i + 128].astype(f32)
            if m == 0:
                block = block * HEAD ** (-0.5)
            turned = block.T.astype(bf16)
            at = slice(144 + HEAD * m, 144 + HEAD * m + HEAD)
            buf[2 * i, at, :] = turned[:HEAD]
            buf[2 * i + 1, at, :] = turned[HEAD:]
        span = pl.ds(2 * i, 2)
        sends.append(pltpu.make_async_copy(buf.at[span], buf_hbm.at[span], out_sem.at[i]))
        sends[-1].start()
    for copy in sends:
        copy.wait()


def chain_kernel(recv, after, send):
    count = recv.shape[0]
    meta = [recv[k, 128:144, :].astype(f32) for k in range(count)]
    gain = [m[1:2, :128] + m[2:3, :128] for m in meta]
    link = [jnp.zeros((1, 128), f32)]
    for k in range(1, count):
        link.append(jnp.where(meta[k][3:4, :128] == meta[k - 1][4:5, :128], 1.0, 0.0))
    state = jnp.zeros((128, 128), f32)
    for k in range(count):
        state = state * link[k]
        send[k, :, 0:128] = state.astype(bf16)
        state = state * gain[k] + recv[k, 0:128, 0:128].astype(f32)
    adjoint = jnp.zeros((128, 128), f32)
    for k in range(count - 1, -1, -1):
        send[k, :, 128:256] = adjoint.astype(bf16)
        adjoint = (adjoint * gain[k] + recv[k, 0:128, 128:256].astype(f32)) * link[k]


def intra_kernel(inp, proj, x, g, te, fs, decay_t, ids, d_out, grad_out, kept, done, mixed):
    done[...] = jnp.zeros(done.shape, f32)
    n_tok = inp.shape[0]
    heads = decay_t.shape[0]
    half = proj.shape[1] // 2
    square = (n_tok, n_tok)
    early, late = iota(square, 0), iota(square, 1)
    run = mm_nt(ones_where(early >= late), decay_t[...])
    run_t = mm(decay_t[...], ones_where(early <= late))
    id_row = ids[...].astype(f32)
    id_col = id_column(id_row)[:, :1]
    bias = jnp.where((early <= late) & (id_col == id_row), 0.0, -1e30)
    b_rows, c_rows = proj[:, :half], proj[:, half:]
    b_dot_c = mm_nt(b_rows, c_rows)
    low_lane = iota((n_tok, 128), 1) < 64
    mixed[...] = jnp.zeros(square, f32)
    for p in range(heads // 2):
        cols = slice(128 * p, 128 * p + 128)
        xp, gp = x[:, cols], g[:, cols]
        zero = jnp.zeros_like(gp)
        total = jnp.zeros((n_tok, 128), f32)
        for k in range(2):
            h = 2 * p + k
            gh = jnp.where(low_lane, gp, zero) if k == 0 else jnp.where(low_lane, zero, gp)
            keep = jnp.exp(run_t[h : h + 1, :] - run[:, h : h + 1] + bias)
            mixed[...] += keep * mm_nt(xp, gh)
            total += mm((keep * b_dot_c).astype(bf16), gh)
        d_out[:, cols] = total
        spread = head_spread(heads, 128, 2 * p)
        rows = slice(n_tok * (p // 2), n_tok * (p // 2) + n_tok)
        side = slice(128 * (p % 2), 128 * (p % 2) + 128)
        kept[0, rows, side] = (xp.astype(f32) * mm(te[...], spread)).astype(bf16)
        kept[1, rows, side] = (gp.astype(f32) * mm(fs[...], spread)).astype(bf16)
        kept[2, cols, :] = inp[:, cols].astype(f32).T.astype(bf16)
    both = mixed[...]
    grad_out[:, :half] = mm(both.astype(bf16), c_rows)
    grad_out[:, half:] = mm(both.T.astype(bf16), b_rows)


def outer_kernel(core, recv_hbm, kept_hbm, grad_in, after, og_out, keep, give, recv, kept, sem):
    owners = recv.shape[0]
    n_tok = grad_in.shape[0]
    copies, arrivals = [], []
    for q in range(4):
        rows = pl.ds(kept.shape[1] // 4 * q, kept.shape[1] // 4)
        for k in range(2):
            copies.append(pltpu.make_async_copy(kept_hbm.at[k, rows], kept.at[k, rows], sem.at[2 * q + k]))
        span = pl.ds(owners // 4 * q, owners // 4)
        arrivals.append(pltpu.make_async_copy(recv_hbm.at[span], recv.at[span], sem.at[9 + q]))
        arrivals[-1].start()
        copies[2 * q].start()
        copies[2 * q + 1].start()
    copies.append(pltpu.make_async_copy(kept_hbm.at[2], kept.at[2], sem.at[8]))
    copies[8].start()
    grad_b = grad_in[:, :128]
    grad_c = grad_in[:, 128:]
    for i in range(owners // 2):
        if i % 2 == 0:
            copies[i].wait()
            copies[i + 1].wait()
            arrivals[i // 2].wait()
        rows = slice(n_tok * i, n_tok * i + n_tok)
        enter = jnp.concatenate([recv[2 * i, :, 0:128], recv[2 * i + 1, :, 0:128]], axis=1)
        leave = jnp.concatenate([recv[2 * i, :, 128:256], recv[2 * i + 1, :, 128:256]], axis=1)
        grad_b += mm_nt(kept[0, rows, :], leave)
        grad_c += mm_nt(kept[1, rows, :], enter)
    og_out[:, :128] = grad_b.astype(bf16)
    og_out[:, 128:] = grad_c.astype(bf16)
    og = og_out[...]
    copies[8].wait()
    rows = kept.shape[1] // owners // 2
    mine = pl.multiple_of(core[0] * rows, rows)
    other = pl.multiple_of(rows - core[0] * rows, rows)
    for first, out in ((mine, keep), (other, give)):
        half = jnp.concatenate([kept[2, pl.ds(2 * rows * j + first, rows), :] for j in range(owners)])
        out[...] = mm(half, og).astype(bf16).reshape(out.shape)


def input_grad_kernel(recv, proj, te, d_in, after, dx_out, done):
    done[...] = jnp.zeros(done.shape, f32)
    owners = recv.shape[0]
    heads = te.shape[1]
    b_rows = proj[:, : proj.shape[1] // 2]
    for i in range(owners // 2):
        cols = slice(256 * i, 256 * i + 256)
        leave = jnp.concatenate([recv[2 * i, :, 128:256], recv[2 * i + 1, :, 128:256]], axis=1)
        spread = mm(te[...], head_spread(heads, 256, 4 * i))
        dx_out[:, cols] = (d_in[:, cols] + spread * mm(b_rows, leave)).astype(bf16)


def attention_kernel(lows, qkv, after, out, done, keys, values, *, begin):
    done[...] = jnp.zeros(done.shape, f32)
    blocks = begin + out.shape[0]
    n = qkv.shape[2]
    slot = iota((16, n), 0).astype(f32)
    zeros48 = jnp.zeros((48, n), f32)

    def prepare(k, carry):
        ids = qkv[k, 128:144, :].astype(f32)[0:1]
        other = jnp.where(ids == slot, 0.0, -BIG)
        tall = jnp.concatenate([qkv[k, 208:272, :].astype(f32), other, zeros48])
        keys[pl.ds(pl.multiple_of(k * n, n), n), :] = tall.T.astype(bf16)
        values[k, 0:64, :] = qkv[k, 272:336, :]
        values[k, 64:80, :] = jnp.ones((16, n), bf16)
        return carry

    lax.fori_loop(lows[begin] // 2 * 2, blocks, prepare, 0)
    later = iota((2 * n, n), 0) - iota((2 * n, n), 1)
    masks = [jnp.where(later > k * n, -BIG, 0.0) for k in range(2)]

    def per_pair(c, carry):
        queries = []
        for k in range(2):
            ids = qkv[2 * c + k, 128:144, :].astype(f32)[0:1]
            own = jnp.where(ids == slot, 1.0, 0.0)
            rows = qkv[2 * c + k, 144:208, :].astype(f32)
            queries.append(jnp.concatenate([rows, own, zeros48]).astype(bf16))

        def scores(at, query):
            return mm(keys[pl.ds(pl.multiple_of(at * n, n), 2 * n), :], query)

        def weighted(at, p):
            return mm(values[at], p[:n]) + mm(values[at + 1], p[n:])

        held = []
        for k in range(2):
            s = scores(2 * c, queries[k]) + masks[k]
            top = jnp.max(s, axis=0, keepdims=True)
            held += [top, weighted(2 * c, jnp.exp(s - top).astype(bf16))]

        def step(i, held):
            at = 2 * (c - i)
            new = []
            s = [scores(at, query) for query in queries]
            for k in range(2):
                top, total = held[2 * k], held[2 * k + 1]
                new_top = jnp.maximum(top, jnp.max(s[k], axis=0, keepdims=True))
                p = jnp.exp(s[k] - new_top).astype(bf16)
                new += [new_top, total * jnp.exp(top - new_top) + weighted(at, p)]
            return tuple(new)

        held = lax.fori_loop(1, c + 1 - lows[2 * c] // 2, step, tuple(held))
        for k in range(2):
            total = held[2 * k + 1]
            out[2 * c + k - begin] = (total[0:64] / total[64:65]).astype(bf16)
        return carry

    lax.fori_loop(begin // 2, blocks // 2, per_pair, 0)


def unpack_kernel(recv, out, done):
    done[...] = jnp.zeros(done.shape, f32)
    for i in range(recv.shape[0] // 2):
        tall = jnp.concatenate([recv[2 * i], recv[2 * i + 1]]).astype(f32)
        out[:, 128 * i : 128 * i + 128] = tall.T.astype(bf16)


def share_sum_kernel(recv, after, passed, out, passed_out):
    total = recv[0].astype(f32)
    for k in range(1, recv.shape[0]):
        total += recv[k].astype(f32)
    out[...] = total.astype(bf16)


def plane_sum_kernel(part, met, after, out):
    total = (part[...].astype(f32) + met[...].astype(f32)).astype(bf16)
    for k in range(out.shape[0]):
        out[k] = total


def assemble_kernel(core, mine, other, out, *, scale):
    for j in range(out.shape[0]):
        out[j, core[0]] = mine[j].astype(f32) * scale
        out[j, 1 - core[0]] = other[j].astype(f32) * scale


def exchange(blocks, axis):
    return lax.all_to_all(blocks, axis, split_axis=0, concat_axis=0, tiled=True)


def per_device(layer_input, proj_weight, ssd_input, log_decay, segment_ids, ssd_cotangent, window_qkv):
    inp, x, g = layer_input[0], ssd_input[0], ssd_cotangent[0]
    decay_t = log_decay[0].T
    qkv = window_qkv[0].transpose(1, 0, 2)
    n_tok, width = inp.shape
    heads = decay_t.shape[0]
    ctx = lax.axis_size("ctx")
    dp = lax.axis_size("dp")
    n_out = proj_weight.shape[1]
    core = lax.axis_index("dp") % 2
    pairs = [(i, i ^ 1) for i in range(dp)]

    done = sds((8, 128), f32)

    vmem = pl.BlockSpec(memory_space=pltpu.VMEM)
    anywhere = pl.BlockSpec(memory_space=pltpu.HBM)
    buf, proj, te, fs = pl.pallas_call(
        front_kernel,
        out_shape=(
            sds((ctx, 336, n_tok), bf16),
            sds((n_tok, n_out), bf16),
            sds((n_tok, heads), bf16),
            sds((n_tok, heads), bf16),
        ),
        in_specs=[anywhere] * 7,
        out_specs=(anywhere, vmem, vmem, vmem),
        scratch_shapes=[
            pltpu.VMEM(a.shape, a.dtype) for a in (inp, proj_weight, x, g, qkv, decay_t, segment_ids)
        ]
        + [
            pltpu.VMEM((ctx, 336, n_tok), bf16),
            pltpu.SemaphoreType.DMA((13,)),
            pltpu.SemaphoreType.DMA((2, 4)),
            pltpu.SemaphoreType.DMA((ctx // 2,)),
        ],
        compiler_params=pltpu.CompilerParams(vmem_limit_bytes=64 << 20),
        cost_estimate=pl.CostEstimate(flops=2 << 30, bytes_accessed=9 << 20, transcendentals=0),
    )(inp, proj_weight, x, g, qkv, decay_t, segment_ids)
    got = exchange(buf, "ctx")

    d_intra, grad_intra, kept, intra_done = call(
        intra_kernel,
        (
            sds((n_tok, width), f32),
            sds((n_tok, n_out), f32),
            sds((3, width, n_tok), bf16),
            done,
        ),
        inp, proj, x, g, te, fs, decay_t, segment_ids,
        scratch=[pltpu.VMEM((n_tok, n_tok), f32)],
        flops=6 << 30, n_bytes=8 << 20,
    )
    sent = call(
        chain_kernel,
        sds((ctx, 128, 256), bf16),
        got, intra_done,
        n_bytes=6 << 20,
    )
    back = exchange(sent, "ctx")

    ids = got[:, 128, :].astype(jnp.int32)
    lows = jnp.sum(ids[None, :, -1] < ids[:, None, 0], axis=1, dtype=jnp.int32)
    def attend(begin, end, after):
        return call(
            functools.partial(attention_kernel, begin=begin),
            (sds((end - begin, HEAD, n_tok), bf16), done),
            lows, got, after,
            scratch=[pltpu.VMEM((end * n_tok, 128), bf16), pltpu.VMEM((end, 80, n_tok), bf16)],
            flops=8 << 30, n_bytes=2 << 20, prefetch=1, hbm=(2,),
        )

    split = ctx * 3 // 8 * 2
    attended, attention_done = attend(0, split, lows)

    half_rows = width // ctx // 2
    out_grad, keep, give = call(
        outer_kernel,
        (sds((n_tok, n_out), bf16), sds((ctx, half_rows, n_out), bf16), sds((ctx, half_rows, n_out), bf16)),
        core[None], back, kept, grad_intra, attention_done,
        scratch=[
            pltpu.VMEM((ctx, 128, 256), bf16),
            pltpu.VMEM((3, width, n_tok), bf16),
            pltpu.SemaphoreType.DMA((13,)),
        ],
        flops=2 << 30, n_bytes=6 << 20, prefetch=1, limit=61 << 20, hbm=(1, 2),
    )
    given = lax.ppermute(give, "dp", pairs)
    share = (keep.astype(f32) + given.astype(f32)).astype(bf16)
    shares = exchange(share, "ctx")
    attended = jnp.concatenate([attended, attend(split, ctx, share[0, :8, :128])[0]])
    input_grad, input_done = call(
        input_grad_kernel,
        (sds((n_tok, width), bf16), done),
        back, proj, te, d_intra, share[0, :8, :128],
        flops=1 << 30, n_bytes=4 << 20, hbm=(4,),
    )
    part, attended = pl.pallas_call(
        share_sum_kernel,
        out_shape=(sds((half_rows, n_out), bf16), sds(attended.shape, bf16)),
        in_specs=[vmem, vmem, anywhere],
        out_specs=(vmem, anywhere),
        input_output_aliases={2: 1},
        compiler_params=pltpu.CompilerParams(vmem_limit_bytes=24 << 20),
        cost_estimate=pl.CostEstimate(flops=0, bytes_accessed=1 << 20, transcendentals=0),
    )(shares, input_done, attended)
    out_rows = exchange(attended, "ctx")
    window_out, window_done = call(
        unpack_kernel, (sds((n_tok, ctx * HEAD), bf16), done), out_rows, n_bytes=1 << 20
    )
    step = 2
    while 2 * step < dp:
        met = lax.ppermute(part, "dp", [(i, i ^ step) for i in range(dp)])
        part = (part.astype(f32) + met.astype(f32)).astype(bf16)
        step *= 2
    met = lax.ppermute(part, "dp", [(i, i ^ step) for i in range(dp)])
    strip = call(plane_sum_kernel, sds((ctx, half_rows, n_out), bf16), part, met, window_done, n_bytes=1 << 20)
    mine = exchange(strip, "ctx")
    other = lax.ppermute(mine, "dp", pairs)
    weight_grad = call(
        functools.partial(assemble_kernel, scale=1.0 / math.sqrt(dp * ctx * n_tok)),
        sds((ctx, 2, half_rows, n_out), f32),
        core[None], mine, other,
        n_bytes=4 << 20, prefetch=1,
    ).reshape(width, n_out)
    return (input_grad[None], out_grad[None], weight_grad, window_out[None])


def solution(mesh):
    placed = (
        P("dp", "ctx", None),
        P(),
        P("dp", "ctx", None),
        P("dp", "ctx", None),
        P("dp", "ctx"),
        P("dp", "ctx", None),
        P("dp", "ctx", None, None),
    )
    return jax.shard_map(
        per_device,
        mesh=mesh,
        in_specs=placed,
        out_specs=(P("dp", "ctx", None), P("dp", "ctx", None), P(), P("dp", "ctx", None)),
        check_vma=False,
    )
```
